32 devices in a mesh: hist: 4 (over z), orow: 2 (over x), ocol: 4 (over y, core).
Axes of the slice: x: 2, y: 2, z: 4, core: 2. Of those that a mesh axis runs over, the one named last changes fastest.
Arguments:
- lesser_hist: float32 [2, 16, 256, 256], P(None, 'hist', 'ocol', 'orow'), may hold values from -6 to 6
- greater_hist: float32 [2, 16, 256, 256], P(None, 'hist', 'orow', 'ocol'), may hold values from -6 to 6
- advanced_hist: float32 [2, 16, 32, 256, 256], P(None, 'hist', 'ocol', None, 'orow'), may hold values from -6 to 6
- current_row: float32 [2, 32, 256, 256], P(None, 'ocol', 'hist', 'orow'), may hold values from -6 to 6
- adjacency: int32 [256, 256], P('hist'), may hold values from 0 to 1, as said below
- weight_table: int32 [16], P('hist'), may hold values from 1 to 48
- step_index: int32 [1], replicated, may hold values from 4 to 15
Outputs:
- new_row: float32 [2, 32, 256, 256], P(None, 'ocol', 'hist', 'orow')
The draws below stay inside these ranges and needn't reach their ends.
Inputs may be any that keep to these rules, and one draw needn't show every extreme that they name: `adjacency`: symmetric, zero on the diagonal.
All inputs are finite; a program needn't handle non-finite values.
Results may differ from the reference program's by a relative error of at most 0.0001.
Values sent between devices are 32-bit elements; how exact they have to be, the bound alone decides.
No kernel may reach another device: no remote copies, remote signals or barrier semaphores. Data moves between devices by JAX's collectives and lax.ppermute only.
A program may use at most 64 MiB of HBM per device.

```python
import jax
import jax.numpy as jnp
from jax import lax

NORB = 256
TPRIME = 32
SLICES = 16


def draw_adjacency(key, part):
    key = jax.random.fold_in(key, 7)
    draws = jax.random.randint(key, (NORB, NORB), 0, NORB)
    upper = jnp.triu((draws < 3).astype(jnp.int32), 1)
    return upper + upper.T


def with_ends(result, stream_key, low, largest):
    place = [jax.random.randint(jax.random.fold_in(stream_key, axis), (), 0, length) for axis, length in enumerate(result.shape)]
    widest = result.shape.index(max(result.shape))
    beside = place[:widest] + [(place[widest] + 1) % result.shape[widest]] + place[widest + 1:]
    return result.at[tuple(place)].set(low).at[tuple(beside)].set(largest)


def steps_of(rng, shape, pieces, low, top_value):
    def one(dim, parts):
        steps = jax.random.uniform(jax.random.fold_in(jax.random.fold_in(rng, 6), dim), (parts,), jnp.float32, low / len(pieces), top_value / len(pieces))
        return jnp.repeat(jnp.exp(steps), shape[dim] // parts).reshape((-1,) + (1,) * (len(shape) - dim - 1))

    gain = one(*pieces[0])
    for cut in pieces[1:]:
        gain = gain * one(*cut)
    return gain


def gaussian(rng, extent, spread, reach, shards=(), kind=jnp.bfloat16):
    values = jax.random.normal(rng, extent, jnp.float32) * spread
    if len(shards) > 0:
        values = steps_of(rng, extent, shards, -0.22, 0.18) * values
    return jnp.clip(values, min=-reach, max=reach).astype(kind)


def setup_inputs(seed: int = 0) -> dict:
    arg_keys = jax.random.split(jax.random.key(seed), 8)
    return {
        "lesser_hist": gaussian(arg_keys[0], (2, SLICES, NORB, NORB), 1.0, 6.0, ((1, 4), (2, 4), (3, 2)), jnp.float32),
        "greater_hist": gaussian(arg_keys[1], (2, SLICES, NORB, NORB), 1.0, 6.0, ((1, 4), (2, 2), (3, 4)), jnp.float32),
        "advanced_hist": gaussian(arg_keys[2], (2, SLICES, TPRIME, NORB, NORB), 1.0, 6.0, ((1, 4), (2, 4), (4, 2)), jnp.float32),
        "current_row": gaussian(arg_keys[3], (2, TPRIME, NORB, NORB), 1.0, 6.0, ((1, 4), (2, 4), (3, 2)), jnp.float32),
        "adjacency": draw_adjacency(jax.random.fold_in(arg_keys[7], 71), 0),
        "weight_table": with_ends(jax.random.randint(arg_keys[5], (SLICES,), 1, 49), jax.random.fold_in(arg_keys[5], 1), 1, 48).astype(jnp.int32),
        "step_index": jax.random.randint(arg_keys[6], (1,), SLICES // 4, SLICES).astype(jnp.int32),
    }


coupling_square = 0.25
hopping = 4.0
time_step = 0.01


def self_energy(lesser, greater_t):
    lesser_re, lesser_im = lesser[0], lesser[1]
    greater_re, greater_im = greater_t[0], greater_t[1]
    square_re = lesser_re * lesser_re - lesser_im * lesser_im
    square_im = 2.0 * lesser_re * lesser_im
    sigma_re = coupling_square * (square_re * greater_re - square_im * greater_im)
    sigma_im = coupling_square * (square_re * greater_im + square_im * greater_re)
    return jnp.stack([sigma_re, sigma_im])


def slice_term(sigma_one, history_one):
    combos = jnp.einsum('cik,dtkj->cdtij', sigma_one, history_one, precision=lax.Precision.HIGHEST, preferred_element_type=jnp.float32)
    return jnp.stack([combos[0, 0] - combos[1, 1], combos[0, 1] + combos[1, 0]])


def reference(lesser_hist, greater_hist, advanced_hist, current_row, adjacency, weight_table, step_index):
    sigma = self_energy(lesser_hist, jnp.swapaxes(greater_hist, 2, 3))
    slot_ids = jnp.arange(SLICES, dtype=jnp.int32)
    weights = jnp.where(slot_ids <= step_index[0], weight_table.astype(jnp.float32) / 24.0, jnp.float32(0.0))
    sigma_w = sigma * weights[None, :, None, None]

    def add_slice(position, accumulated):
        sigma_one = lax.dynamic_index_in_dim(sigma_w, position, 1, keepdims=False)
        history_one = lax.dynamic_index_in_dim(advanced_hist, position, 1, keepdims=False)
        return accumulated + slice_term(sigma_one, history_one)

    start = jnp.zeros((2, TPRIME, NORB, NORB), jnp.float32)
    collision = lax.fori_loop(0, SLICES, add_slice, start)
    hop_matrix = -hopping * adjacency.astype(jnp.float32)
    hop_term = jnp.einsum('ik,ctkj->ctij', hop_matrix, current_row, precision=lax.Precision.HIGHEST, preferred_element_type=jnp.float32)
    summed = collision + hop_term
    return jnp.stack([current_row[0] + time_step * summed[1], current_row[1] - time_step * summed[0]])
```

```python
import functools

import jax
import jax.numpy as jnp
from jax import lax
from jax.experimental import pallas as pl
from jax.experimental.pallas import tpu as pltpu
from jax.sharding import PartitionSpec as P

coupling_square = 0.25
hopping = 4.0
time_step = 0.01
CHUNKS = 4


def sigma_kernel(weights_ref, lesser_ref, greater_ref, out_ref):
    for s in range(lesser_ref.shape[1]):
        a_re, a_im = lesser_ref[0, s], lesser_ref[1, s]
        b_re, b_im = greater_ref[0, s].T, greater_ref[1, s].T
        square_re = a_re * a_re - a_im * a_im
        square_im = 2.0 * a_re * a_im
        scale = coupling_square * weights_ref[s]
        out_ref[0, s] = scale * (square_re * b_re - square_im * b_im)
        out_ref[1, s] = scale * (square_re * b_im + square_im * b_re)


def split(x):
    high = x.astype(jnp.bfloat16)
    return high, (x - high.astype(jnp.float32)).astype(jnp.bfloat16)


def chunk_kernel(masks, ends, where_ref, *refs):
    count = len(masks)
    blocks, refs = refs[:count], refs[count:]
    advanced_ref, row_ref, adjacency_ref = refs[:3]
    outs, (left_high, left_low, result) = refs[3:-3], refs[-3:]
    slices = advanced_ref.shape[1]
    my_orow, my_ocol, my_hist = where_ref[0], where_ref[1], where_ref[2]

    @pl.when(pl.program_id(0) == 0)
    def _():
        for (flip_orow, flip_ocol), block in zip(masks, blocks):
            at_orow = jnp.bitwise_xor(my_orow, flip_orow)
            at_ocol = jnp.bitwise_xor(my_ocol, flip_ocol)
            for s in range(slices):
                for part in range(2):
                    high, low = split(block[part, s])
                    left_high[s, at_orow, part, at_ocol] = high
                    left_low[s, at_orow, part, at_ocol] = low

    norb = advanced_ref.shape[3]
    width = advanced_ref.shape[4]
    halves = left_high.shape[1]

    def left(ref, s):
        return jnp.concatenate([ref[s, half].reshape(2 * norb, norb // halves) for half in range(halves)], axis=1)

    total = None
    for s in range(slices):
        right = jnp.concatenate([advanced_ref[0, s, 0], advanced_ref[1, s, 0]], axis=1)
        right_high, right_low = split(right)
        here = jnp.dot(
            jnp.concatenate([left(left_high, s), left(left_high, s), left(left_low, s)], axis=1),
            jnp.concatenate([right_high, right_low, right_high], axis=0),
            preferred_element_type=jnp.float32,
        )
        total = here if total is None else total + here
    hop = lax.dot_general(
        -hopping * adjacency_ref[...].astype(jnp.float32),
        jnp.concatenate([row_ref[0, 0], row_ref[1, 0]], axis=1),
        (((0,), (0,)), ((), ())),
        precision=lax.Precision.HIGHEST,
        preferred_element_type=jnp.float32,
    )
    sum_re = total[:norb, :width] - total[norb:, width:] + hop[:, :width]
    sum_im = total[:norb, width:] + total[norb:, :width] + hop[:, width:]
    if not ends:
        outs[0][0, 0] = sum_re
        outs[0][1, 0] = sum_im
        return
    rows = norb // len(outs)
    for block in range(len(outs)):
        result[block, 0] = sum_re[block * rows : (block + 1) * rows]
        result[block, 1] = sum_im[block * rows : (block + 1) * rows]
    for place, out in enumerate(outs):
        block = jnp.where(my_hist < len(outs) // 2, len(outs) - 1 - place, place)
        out[0, 0] = result[block, 0]
        out[1, 0] = result[block, 1]


def on_device(
    hist_size, orow_size, ocol_size, lesser_hist, greater_hist, advanced_hist, current_row, adjacency, weight_table, step_index
):
    slices = lesser_hist.shape[1]
    my_hist, my_orow, my_ocol = lax.axis_index("hist"), lax.axis_index("orow"), lax.axis_index("ocol")
    slot_ids = my_hist * slices + lax.iota(jnp.int32, slices)
    weights = jnp.where(
        slot_ids <= step_index[0], weight_table.astype(jnp.float32) / 24.0, jnp.float32(0.0)
    )
    vmem = pl.BlockSpec(memory_space=pltpu.VMEM)
    smem = pl.BlockSpec(memory_space=pltpu.SMEM)
    sigma = pl.pallas_call(
        sigma_kernel,
        out_shape=jax.ShapeDtypeStruct(lesser_hist.shape, jnp.float32),
        in_specs=[smem, vmem, vmem],
        out_specs=vmem,
        name="sigma",
    )(weights, lesser_hist, greater_hist)

    def flipped(x, flip_orow, flip_ocol):
        pairs = [
            (r * ocol_size + c, (r ^ flip_orow) * ocol_size + (c ^ flip_ocol))
            for r in range(orow_size)
            for c in range(ocol_size)
        ]
        return lax.ppermute(x, ("orow", "ocol"), pairs)

    masks = [(r, c) for c in range(0, ocol_size, 2) for r in range(orow_size)]
    held = {mask: sigma if mask == (0, 0) else flipped(sigma, *mask) for mask in masks}
    for r, c in masks:
        held[(r, c + 1)] = flipped(held[(r, c)], 0, 1)
    masks = tuple(held)

    times, norb, width = advanced_hist.shape[2:]
    each = times // CHUNKS
    rows = norb // hist_size
    line = hist_size == 4
    where = jnp.stack([my_orow, my_ocol, my_hist]).astype(jnp.int32)
    block_shape = lesser_hist.shape
    pieces = []
    for chunk in range(CHUNKS):
        if line:
            out_shape = [jax.ShapeDtypeStruct((2, each, rows, width), jnp.float32)] * hist_size
            out_specs = [pl.BlockSpec((2, 1, rows, width), lambda t: (0, t, 0, 0))] * hist_size
        else:
            out_shape = [jax.ShapeDtypeStruct((2, each, norb, width), jnp.float32)]
            out_specs = [pl.BlockSpec((2, 1, norb, width), lambda t: (0, t, 0, 0))]
        first = chunk * each
        parts = pl.pallas_call(
            functools.partial(chunk_kernel, masks, line),
            grid=(each,),
            out_shape=out_shape,
            in_specs=[smem]
            + [pl.BlockSpec(block_shape, lambda t: (0, 0, 0, 0))] * len(masks)
            + [
                pl.BlockSpec((2, slices, 1, norb, width), lambda t, first=first: (0, 0, first + t, 0, 0)),
                pl.BlockSpec((2, 1, current_row.shape[2], width), lambda t, first=first: (0, first + t, 0, 0)),
                pl.BlockSpec(adjacency.shape, lambda t: (0, 0)),
            ],
            out_specs=out_specs,
            scratch_shapes=[
                pltpu.VMEM((slices, orow_size, 2, ocol_size) + block_shape[2:], jnp.bfloat16),
                pltpu.VMEM((slices, orow_size, 2, ocol_size) + block_shape[2:], jnp.bfloat16),
                pltpu.VMEM((hist_size, 2, rows, width), jnp.float32),
            ],
            compiler_params=pltpu.CompilerParams(vmem_limit_bytes=40 * 1024 * 1024),
            name=f"products_{chunk}",
        )(where, *[held[mask] for mask in masks], advanced_hist, current_row, adjacency)
        if not line:
            pieces.append(lax.psum_scatter(parts[0], "hist", scatter_dimension=2, tiled=True))
            continue
        inward = [lax.ppermute(part, "hist", [(0, 1), (3, 2)]) for part in parts[:3]]
        across = [lax.ppermute(parts[m] + inward[m], "hist", [(1, 2), (2, 1)]) for m in range(2)]
        outward = lax.ppermute(parts[3] + across[0], "hist", [(2, 3), (1, 0)])
        at_end = jnp.logical_or(my_hist == 0, my_hist == hist_size - 1)
        pieces.append(jnp.where(at_end, parts[3] + outward, parts[2] + inward[2] + across[1]))
    summed = jnp.concatenate(pieces, axis=1)
    return jnp.stack(
        [current_row[0] + time_step * summed[1], current_row[1] - time_step * summed[0]]
    )


def solution(mesh):
    in_specs = (
        P(None, "hist", "ocol", "orow"),
        P(None, "hist", "orow", "ocol"),
        P(None, "hist", "ocol", None, "orow"),
        P(None, "ocol", "hist", "orow"),
        P("hist", None),
        P("hist"),
        P(),
    )
    out_specs = P(None, "ocol", "hist", "orow")
    body = functools.partial(on_device, mesh.shape["hist"], mesh.shape["orow"], mesh.shape["ocol"])
    return jax.shard_map(
        body, mesh=mesh, in_specs=in_specs, out_specs=out_specs, check_vma=False
    )
```

```python
import functools

import jax
import jax.numpy as jnp
from jax import lax
from jax.experimental import pallas as pl
from jax.experimental.pallas import tpu as pltpu
from jax.sharding import PartitionSpec as P

coupling_square = 0.25
hopping = 4.0
time_step = 0.01
CHUNKS = 4
VMEM = pl.BlockSpec(memory_space=pltpu.VMEM)
SMEM = pl.BlockSpec(memory_space=pltpu.SMEM)
HBM = pl.BlockSpec(memory_space=pltpu.HBM)


def sigma_kernel(hist_ref, table_ref, step_ref, lesser_hbm, greater_hbm, out_ref, lesser, greater, sems):
    slices = lesser.shape[1]
    copies = [
        pltpu.make_async_copy(lesser_hbm, lesser, sems.at[0]),
        pltpu.make_async_copy(greater_hbm, greater, sems.at[1]),
    ]
    for copy in copies:
        copy.start()
    for copy in copies:
        copy.wait()
    for s in range(slices):
        numerator = jnp.full((1, lesser.shape[3]), table_ref[s], jnp.int32).astype(jnp.float32)
        weight = jnp.where(hist_ref[0] * slices + s <= step_ref[0], numerator / 24.0, 0.0)
        a_re, a_im = lesser[0, s], lesser[1, s]
        b_re, b_im = greater[0, s], greater[1, s]
        square_re = a_re * a_re - a_im * a_im
        square_im = 2.0 * a_re * a_im
        scale = coupling_square * weight
        out_ref[0, s] = scale * (square_re * b_re - square_im * b_im)
        out_ref[1, s] = scale * (square_re * b_im + square_im * b_re)


def split(x):
    high = x.astype(jnp.bfloat16)
    return high, (x - high.astype(jnp.float32)).astype(jnp.bfloat16)


def history_kernel(
    advanced_hbm, row_hbm, adjacency_hbm, high_ref, low_ref, hop_ref, row, advanced, adjacency, sems
):
    slices, width = advanced.shape[2], advanced.shape[4]
    times = row.shape[1]
    each = times // high_ref.shape[0]

    def fetch(t):
        return pltpu.make_async_copy(advanced_hbm.at[:, :, t], advanced.at[t % 2], sems.at[t % 2])

    small = [
        pltpu.make_async_copy(row_hbm, row, sems.at[2]),
        pltpu.make_async_copy(adjacency_hbm, adjacency, sems.at[3]),
    ]
    for copy in small:
        copy.start()
    fetch(0).start()
    fetch(1).start()
    for copy in small:
        copy.wait()
    graph = (-hopping * adjacency[...].astype(jnp.float32)).T.astype(jnp.bfloat16)
    for t in range(times):
        chunk, place = t // each, (t % each) * 2 * width
        row_high, row_low = split(jnp.concatenate([row[0, t], row[1, t]], axis=1))
        hop_ref[chunk, :, place : place + 2 * width] = jnp.dot(
            graph, row_high, preferred_element_type=jnp.float32
        ) + jnp.dot(graph, row_low, preferred_element_type=jnp.float32)
        fetch(t).wait()
        for s in range(slices):
            for part in range(2):
                high, low = split(advanced[t % 2, part, s])
                high_ref[chunk, s, :, place + part * width : place + (part + 1) * width] = high
                low_ref[chunk, s, :, place + part * width : place + (part + 1) * width] = low
        if t + 2 < times:
            fetch(t + 2).start()


def assemble(masks, my_orow, my_ocol, blocks, left_high, left_low):
    for (flip_orow, flip_ocol), block in zip(masks, blocks):
        at_orow = jnp.bitwise_xor(my_orow, flip_orow)
        at_ocol = jnp.bitwise_xor(my_ocol, flip_ocol)
        for s in range(left_high.shape[0]):
            for part in range(2):
                high, low = split(block[part, s])
                left_high[s, at_orow, part, at_ocol] = high
                left_low[s, at_orow, part, at_ocol] = low


def chunk_kernel(chunk, masks, ring, hist_ref, orow_ref, ocol_ref, right_high, right_low, hop_ref, *refs):
    if masks:
        blocks, refs = refs[: len(masks)], refs[len(masks) :]
        left_high, left_low, outs, result = refs[-3], refs[-2], refs[:-3], refs[-1]
        assemble(masks, orow_ref[0], ocol_ref[0], blocks, left_high, left_low)
    else:
        left_high, left_low, outs, result = refs[0], refs[1], refs[2:-1], refs[-1]
    slices, halves = left_high.shape[:2]
    norb = right_high.shape[2]
    width = outs[0].shape[3]

    def left(ref, s):
        return jnp.concatenate([ref[s, half].reshape(2 * norb, norb // halves) for half in range(halves)], axis=1)

    total = None
    for s in range(slices):
        high = right_high[chunk, s]
        here = jnp.dot(
            jnp.concatenate([left(left_high, s), left(left_high, s), left(left_low, s)], axis=1),
            jnp.concatenate([high, right_low[chunk, s], high], axis=0),
            preferred_element_type=jnp.float32,
        )
        total = here if total is None else total + here
    for t in range(outs[0].shape[1]):
        at = 2 * width * t
        sum_re = total[:norb, at : at + width] - total[norb:, at + width : at + 2 * width] + hop_ref[chunk, :, at : at + width]
        sum_im = total[:norb, at + width : at + 2 * width] + total[norb:, at : at + width] + hop_ref[chunk, :, at + width : at + 2 * width]
        if not ring:
            outs[0][0, t] = sum_re
            outs[0][1, t] = sum_im
            continue
        rows = norb // len(ring)
        for block in range(len(ring)):
            result[t, block, 0] = sum_re[block * rows : (block + 1) * rows]
            result[t, block, 1] = sum_im[block * rows : (block + 1) * rows]
    if not ring:
        return
    size = len(ring)
    my_hist = hist_ref[0]
    my_place = sum(jnp.where(my_hist == h, ring.index(h), 0) for h in range(size))
    for step, out in enumerate(outs):
        place = my_place + (size - 1 - step)
        place = jnp.where(place >= size, place - size, place)
        block = sum(jnp.where(place == p, ring[p], 0) for p in range(size))
        for t in range(out.shape[1]):
            out[0, t] = result[t, block, 0]
            out[1, t] = result[t, block, 1]


def step_kernel(*refs):
    chunks = (len(refs) - 4) // 2
    arrived, own = refs[:chunks], refs[chunks : 2 * chunks]
    row, out_hbm, out, sems = refs[2 * chunks :]
    each = own[0].shape[1]
    copies = []
    for chunk in range(chunks):
        here = pl.ds(chunk * each, each)
        summed_re = arrived[chunk][0] + own[chunk][0]
        summed_im = arrived[chunk][1] + own[chunk][1]
        out[0, here] = row[0, here] + time_step * summed_im
        out[1, here] = row[1, here] - time_step * summed_re
        copies.append(pltpu.make_async_copy(out.at[:, here], out_hbm.at[:, here], sems.at[chunk]))
        copies[-1].start()
    for copy in copies:
        copy.wait()


def ring_of(size):
    return [place for place in range(size) if place == 0 or place % 2 == 1] + [
        place for place in range(size - 1, 0, -1) if place % 2 == 0
    ]


def limit(mebibytes):
    return pltpu.CompilerParams(vmem_limit_bytes=mebibytes * 1024 * 1024)


def in_vmem(x):
    return pltpu.with_memory_space_constraint(x, pltpu.VMEM)


def in_hbm(x):
    return pltpu.with_memory_space_constraint(x, pltpu.HBM)


def on_device(
    hist_size, orow_size, ocol_size, lesser_hist, greater_hist, advanced_hist, current_row, adjacency, weight_table, step_index
):
    slices, times, norb, width = advanced_hist.shape[1:]
    block = lesser_hist.shape
    my_hist, my_orow, my_ocol = lax.axis_index("hist"), lax.axis_index("orow"), lax.axis_index("ocol")
    me = [index.reshape(1).astype(jnp.int32) for index in (my_hist, my_orow, my_ocol)]
    sigma = pl.pallas_call(
        sigma_kernel,
        out_shape=pltpu.VMEM(block, jnp.float32),
        in_specs=[SMEM, SMEM, SMEM, HBM, HBM],
        out_specs=VMEM,
        scratch_shapes=[
            pltpu.VMEM(block, jnp.float32),
            pltpu.VMEM(block, jnp.float32),
            pltpu.SemaphoreType.DMA((2,)),
        ],
        compiler_params=limit(4),
        name="sigma",
    )(me[0], weight_table, step_index, in_hbm(lesser_hist), in_hbm(jnp.swapaxes(greater_hist, 2, 3)))

    each = times // CHUNKS
    right_high, right_low, hop, row = pl.pallas_call(
        history_kernel,
        out_shape=[
            pltpu.VMEM((CHUNKS, slices, norb, each * 2 * width), jnp.bfloat16),
            pltpu.VMEM((CHUNKS, slices, norb, each * 2 * width), jnp.bfloat16),
            pltpu.VMEM((CHUNKS, norb, each * 2 * width), jnp.float32),
            pltpu.VMEM(current_row.shape, jnp.float32),
        ],
        in_specs=[HBM, HBM, HBM],
        out_specs=[VMEM] * 4,
        scratch_shapes=[
            pltpu.VMEM((2, 2, slices, norb, width), jnp.float32),
            pltpu.VMEM(adjacency.shape, jnp.int32),
            pltpu.SemaphoreType.DMA((4,)),
        ],
        cost_estimate=pl.CostEstimate(flops=0, bytes_accessed=16 * 1024 * 1024, transcendentals=0),
        compiler_params=limit(16),
        name="history",
    )(in_hbm(advanced_hist), in_hbm(current_row), in_hbm(adjacency))

    def moved(x, target):
        pairs = [
            (r * ocol_size + c, target(r, c)[0] * ocol_size + target(r, c)[1])
            for r in range(orow_size)
            for c in range(ocol_size)
        ]
        return lax.ppermute(x, ("orow", "ocol"), pairs)

    held = {(0, 0): sigma}
    held[(1, 0)] = moved(sigma, lambda r, c: (r ^ 1, c))
    held[(0, 2)] = moved(sigma, lambda r, c: (r, c ^ 2))
    held[(0, 1)] = moved(sigma, lambda r, c: (r, c ^ 1))
    over_orow, over_ocol, hop = lax.optimization_barrier((held[(1, 0)], held[(0, 2)], hop))
    passed_on = jnp.where(my_ocol % 2 == 0, over_orow, over_ocol)
    held[(1, 2)] = moved(passed_on, lambda r, c: (r, c ^ 2) if c % 2 == 0 else (r ^ 1, c))
    for r, c in ((1, 0), (0, 2), (1, 2)):
        held[(r, c + 1)] = moved(held[(r, c)], lambda r, c: (r, c ^ 1))
    masks = tuple(held)

    rows = norb // hist_size
    ring = ring_of(hist_size) if hist_size <= 8 else []
    left_shape = (slices, orow_size, 2, ocol_size) + block[2:]
    left = None
    arrived, own, first_come = [], [], []
    for chunk in range(CHUNKS):
        if ring:
            out_shape = [pltpu.VMEM((2, each, rows, width), jnp.float32)] * hist_size
        else:
            out_shape = [pltpu.VMEM((2, each, norb, width), jnp.float32)]
        after = me
        if chunk >= 2 and ring:
            after = me[:2] + [lax.optimization_barrier((me[2], first_come[chunk - 2]))[0]]
        if left is None:
            operands, extra = [in_vmem(held[mask]) for mask in masks], [pltpu.VMEM(left_shape, jnp.bfloat16)] * 2
        else:
            operands, extra = [in_vmem(x) for x in left], []
        parts = pl.pallas_call(
            functools.partial(chunk_kernel, chunk, masks if left is None else (), ring),
            out_shape=out_shape + extra,
            in_specs=[SMEM] * 3 + [VMEM] * (3 + len(operands)),
            out_specs=[VMEM] * (len(out_shape) + len(extra)),
            scratch_shapes=[pltpu.VMEM((each, hist_size, 2, rows, width), jnp.float32)],
            cost_estimate=pl.CostEstimate(
                flops=6 * each * slices * 2 * norb * norb * 2 * width, bytes_accessed=0, transcendentals=0
            ),
            compiler_params=limit(16),
            name=f"products_{chunk}",
        )(*after, in_vmem(right_high), in_vmem(right_low), in_vmem(hop), *operands)
        if left is None:
            left, parts = parts[-2:], parts[:-2]
        if not ring:
            total = lax.psum_scatter(parts[0], "hist", scatter_dimension=2, tiled=True)
            arrived.append(total)
            own.append(jnp.zeros_like(total))
            continue
        pairs = [(ring[p], ring[(p + 1) % hist_size]) for p in range(hist_size)]
        moving = parts[0]
        for m in range(1, hist_size):
            moving = lax.ppermute(moving, "hist", pairs)
            if m == 1:
                first_come.append(moving)
            if m < hist_size - 1:
                moving = moving + parts[m]
        arrived.append(moving)
        own.append(parts[-1])
    return pl.pallas_call(
        step_kernel,
        out_shape=jax.ShapeDtypeStruct(current_row.shape, jnp.float32),
        in_specs=[VMEM] * (2 * CHUNKS + 1),
        out_specs=HBM,
        scratch_shapes=[pltpu.VMEM(current_row.shape, jnp.float32), pltpu.SemaphoreType.DMA((CHUNKS,))],
        compiler_params=limit(4),
        name="step",
    )(*[in_vmem(x) for x in arrived], *[in_vmem(x) for x in own], in_vmem(row))


def solution(mesh):
    in_specs = (
        P(None, "hist", "ocol", "orow"),
        P(None, "hist", "orow", "ocol"),
        P(None, "hist", "ocol", None, "orow"),
        P(None, "ocol", "hist", "orow"),
        P("hist", None),
        P("hist"),
        P(),
    )
    out_specs = P(None, "ocol", "hist", "orow")
    body = functools.partial(on_device, mesh.shape["hist"], mesh.shape["orow"], mesh.shape["ocol"])
    return jax.shard_map(
        body, mesh=mesh, in_specs=in_specs, out_specs=out_specs, check_vma=False
    )
```

```python
import functools

import jax
import jax.numpy as jnp
from jax import lax
from jax.experimental import pallas as pl
from jax.experimental.pallas import tpu as pltpu
from jax.sharding import PartitionSpec as P

coupling_square = 0.25
hopping = 4.0
time_step = 0.01
VMEM = pl.BlockSpec(memory_space=pltpu.VMEM)
SMEM = pl.BlockSpec(memory_space=pltpu.SMEM)
HBM = pl.BlockSpec(memory_space=pltpu.HBM)


def sigma_kernel(hist_ref, step_ref, table_hbm, lesser_hbm, greater_hbm, out_ref, lesser, greater, table_ref, sems):
    slices = lesser.shape[1]
    copies = [
        pltpu.make_async_copy(source, target, sems.at[place])
        for place, (source, target) in enumerate(
            [(table_hbm, table_ref), (lesser_hbm, lesser), (greater_hbm, greater)]
        )
    ]
    for copy in copies:
        copy.start()
    for copy in copies:
        copy.wait()
    for s in range(slices):
        numerator = jnp.full((1, lesser.shape[3]), table_ref[s], jnp.int32).astype(jnp.float32)
        weight = jnp.where(hist_ref[0] * slices + s <= step_ref[0], numerator / 24.0, 0.0)
        a_re, a_im = lesser[0, s], lesser[1, s]
        b_re, b_im = greater[0, s], greater[1, s]
        square_re = a_re * a_re - a_im * a_im
        square_im = 2.0 * a_re * a_im
        scale = coupling_square * weight
        out_ref[0, s] = scale * (square_re * b_re - square_im * b_im)
        out_ref[1, s] = scale * (square_re * b_im + square_im * b_re)


def split(x):
    high = x.astype(jnp.bfloat16)
    return high, (x - high.astype(jnp.float32)).astype(jnp.bfloat16)


def history_kernel(
    first, advanced_hbm, row_hbm, adjacency_hbm, high_ref, low_ref, hop_ref, row, advanced, adjacency, sems
):
    slices, each, width = advanced.shape[1], advanced.shape[2], advanced.shape[4]
    near = [
        pltpu.make_async_copy(row_hbm.at[:, pl.ds(first, each)], row, sems.at[each]),
        pltpu.make_async_copy(adjacency_hbm, adjacency, sems.at[each + 1]),
    ]
    far = [
        pltpu.make_async_copy(advanced_hbm.at[:, :, first + t], advanced.at[:, :, t], sems.at[t]) for t in range(each)
    ]
    for copy in near + far:
        copy.start()
    for copy in near:
        copy.wait()
    graph = (-hopping * adjacency[...].astype(jnp.float32)).T.astype(jnp.bfloat16)
    for t in range(each):
        place = t * 2 * width
        row_high, row_low = split(jnp.concatenate([row[0, t], row[1, t]], axis=1))
        hop_ref[:, place : place + 2 * width] = jnp.dot(
            graph, row_high, preferred_element_type=jnp.float32
        ) + jnp.dot(graph, row_low, preferred_element_type=jnp.float32)
    for t in range(each):
        far[t].wait()
        for s in range(slices):
            for part in range(2):
                place = (2 * t + part) * width
                high, low = split(advanced[part, s, t])
                high_ref[s, :, place : place + width] = high
                low_ref[s, :, place : place + width] = low


def assemble(masks, my_orow, my_ocol, blocks, left_high, left_low):
    for (flip_orow, flip_ocol), block in zip(masks, blocks):
        at_orow = jnp.bitwise_xor(my_orow, flip_orow)
        at_ocol = jnp.bitwise_xor(my_ocol, flip_ocol)
        for s in range(left_high.shape[0]):
            for part in range(2):
                high, low = split(block(part, s) if callable(block) else block[part, s])
                left_high[s, at_orow, part, at_ocol] = high
                left_low[s, at_orow, part, at_ocol] = low


def assemble_kernel(masks, orow_ref, ocol_ref, *refs):
    assemble(masks, orow_ref[0], ocol_ref[0], refs[:-3], refs[-3], refs[-2])
    refs[-1][...] = jnp.zeros_like(refs[-1])


def halves_kernel(first_ref, second_ref, first_half, second_half):
    slices = first_half.shape[1]
    first_half[...] = first_ref[:, :slices]
    second_half[...] = second_ref[:, slices:]


def join(halves):
    half = halves[0].shape[1]
    return lambda part, s: halves[s // half][part, s % half]


def chunk_kernel(masks, ring, hist_ref, orow_ref, ocol_ref, right_high, right_low, hop_ref, left_high, left_low, *refs):
    outs, result = refs[2 * len(masks) : -1], refs[-1]
    if masks:
        left_high, left_low, outs = outs[-2], outs[-1], outs[:-2]
        blocks = [join(refs[2 * place : 2 * place + 2]) for place in range(len(masks))]
        assemble(masks, orow_ref[0], ocol_ref[0], blocks, left_high, left_low)
    slices, halves = left_high.shape[:2]
    norb = right_high.shape[1]
    width = outs[0].shape[3]

    def left(ref, s):
        return jnp.concatenate([ref[s, half].reshape(2 * norb, norb // halves) for half in range(halves)], axis=1)

    total = None
    for s in range(slices):
        high = right_high[s]
        here = jnp.dot(
            jnp.concatenate([left(left_high, s), left(left_high, s), left(left_low, s)], axis=1),
            jnp.concatenate([high, right_low[s], high], axis=0),
            preferred_element_type=jnp.float32,
        )
        total = here if total is None else total + here
    for t in range(outs[0].shape[1]):
        at = 2 * width * t
        sum_re = total[:norb, at : at + width] - total[norb:, at + width : at + 2 * width] + hop_ref[:, at : at + width]
        sum_im = total[:norb, at + width : at + 2 * width] + total[norb:, at : at + width] + hop_ref[:, at + width : at + 2 * width]
        if not ring:
            outs[0][0, t] = sum_re
            outs[0][1, t] = sum_im
            continue
        rows = norb // len(ring)
        for block in range(len(ring)):
            result[t, block, 0] = sum_re[block * rows : (block + 1) * rows]
            result[t, block, 1] = sum_im[block * rows : (block + 1) * rows]
    if not ring:
        return
    size = len(ring)
    my_hist = hist_ref[0]
    my_place = sum(jnp.where(my_hist == h, ring.index(h), 0) for h in range(size))
    for step, out in enumerate(outs):
        place = my_place + (size - 1 - step)
        place = jnp.where(place >= size, place - size, place)
        block = sum(jnp.where(place == p, ring[p], 0) for p in range(size))
        for t in range(out.shape[1]):
            out[0, t] = result[t, block, 0]
            out[1, t] = result[t, block, 1]


def step_kernel(*refs):
    chunks = (len(refs) - 3) // 3
    arrived, own, row = refs[:chunks], refs[chunks : 2 * chunks], refs[2 * chunks : 3 * chunks]
    out_hbm, out, sems = refs[3 * chunks :]
    copies, first = [], 0
    for chunk in range(chunks):
        here = pl.ds(first, own[chunk].shape[1])
        first += own[chunk].shape[1]
        out[0, here] = row[chunk][0] + time_step * (arrived[chunk][1] + own[chunk][1])
        out[1, here] = row[chunk][1] - time_step * (arrived[chunk][0] + own[chunk][0])
        copies.append(pltpu.make_async_copy(out.at[:, here], out_hbm.at[:, here], sems.at[chunk]))
        copies[-1].start()
    for copy in copies:
        copy.wait()


def ring_of(size):
    return [place for place in range(size) if place == 0 or place % 2 == 1] + [
        place for place in range(size - 1, 0, -1) if place % 2 == 0
    ]


def limit(mebibytes):
    return pltpu.CompilerParams(vmem_limit_bytes=mebibytes * 1024 * 1024)


def in_vmem(x):
    return pltpu.with_memory_space_constraint(x, pltpu.VMEM)


def in_hbm(x):
    return pltpu.with_memory_space_constraint(x, pltpu.HBM)


def on_device(
    hist_size, orow_size, ocol_size, lesser_hist, greater_hist, advanced_hist, current_row, adjacency, weight_table, step_index
):
    slices, times, norb, width = advanced_hist.shape[1:]
    block = lesser_hist.shape
    my_hist, my_orow, my_ocol = lax.axis_index("hist"), lax.axis_index("orow"), lax.axis_index("ocol")
    me = [index.reshape(1).astype(jnp.int32) for index in (my_hist, my_orow, my_ocol)]
    sigma = pl.pallas_call(
        sigma_kernel,
        out_shape=pltpu.VMEM(block, jnp.float32),
        in_specs=[SMEM] * 2 + [HBM] * 3,
        out_specs=VMEM,
        scratch_shapes=[
            pltpu.VMEM(block, jnp.float32),
            pltpu.VMEM(block, jnp.float32),
            pltpu.SMEM(weight_table.shape, jnp.int32),
            pltpu.SemaphoreType.DMA((3,)),
        ],
        compiler_params=limit(4),
        name="sigma",
    )(me[0], step_index, in_hbm(weight_table), in_hbm(lesser_hist), in_hbm(jnp.swapaxes(greater_hist, 2, 3)))

    short = times // 4
    sizes = [short, (times - short) // 2, times - short - (times - short) // 2]
    chunks = len(sizes)

    def history(chunk):
        each = sizes[chunk]
        return list(pl.pallas_call(
            functools.partial(history_kernel, sum(sizes[:chunk])),
            out_shape=[
                pltpu.VMEM((slices, norb, each * 2 * width), jnp.bfloat16),
                pltpu.VMEM((slices, norb, each * 2 * width), jnp.bfloat16),
                pltpu.VMEM((norb, each * 2 * width), jnp.float32),
                pltpu.VMEM((2, each) + current_row.shape[2:], jnp.float32),
            ],
            in_specs=[HBM] * 3,
            out_specs=[VMEM] * 4,
            scratch_shapes=[
                pltpu.VMEM((2, slices, each, norb, width), jnp.float32),
                pltpu.VMEM(adjacency.shape, jnp.int32),
                pltpu.SemaphoreType.DMA((each + 2,)),
            ],
            compiler_params=limit(12),
            cost_estimate=pl.CostEstimate(flops=0, bytes_accessed=4 * 1024 * 1024, transcendentals=0),
            name=f"history_{chunk}",
        )(in_hbm(advanced_hist), in_hbm(current_row), in_hbm(adjacency)))

    def moved(x, target):
        pairs = [
            (r * ocol_size + c, target(r, c)[0] * ocol_size + target(r, c)[1])
            for r in range(orow_size)
            for c in range(ocol_size)
        ]
        return lax.ppermute(x, ("orow", "ocol"), pairs)

    def over_core(x):
        return moved(x, lambda r, c: (r, c ^ 1))

    histories = [history(chunk) for chunk in range(chunks)]
    held = {(0, 0): sigma}
    held[(1, 0)] = moved(sigma, lambda r, c: (r ^ 1, c))
    held[(0, 2)] = moved(sigma, lambda r, c: (r, c ^ 2))
    held[(0, 1)] = over_core(sigma)
    over_orow, over_ocol, *_ = lax.optimization_barrier(
        (held[(1, 0)], held[(0, 2)], histories[0][3], histories[1][3])
    )
    half_shape = (2, slices // 2) + block[2:]
    halves = pl.pallas_call(
        halves_kernel,
        out_shape=[pltpu.VMEM(half_shape, jnp.float32), pltpu.VMEM((2, slices - slices // 2) + block[2:], jnp.float32)],
        in_specs=[VMEM] * 2,
        out_specs=[VMEM] * 2,
        compiler_params=limit(4),
        name="halves",
    )(in_vmem(over_orow), in_vmem(over_ocol))
    late = (moved(halves[0], lambda r, c: (r, c ^ 2)), moved(halves[1], lambda r, c: (r ^ 1, c)))
    held[(1, 1)] = over_core(held[(1, 0)])
    held[(0, 3)] = over_core(held[(0, 2)])
    left_shape = (slices, orow_size, 2, ocol_size) + block[2:]
    *left, token = pl.pallas_call(
        functools.partial(assemble_kernel, tuple(held)),
        out_shape=[pltpu.VMEM(left_shape, jnp.bfloat16)] * 2 + [pltpu.VMEM((8, 128), jnp.float32)],
        in_specs=[SMEM] * 2 + [VMEM] * len(held),
        out_specs=[VMEM] * 3,
        compiler_params=limit(4),
        cost_estimate=pl.CostEstimate(flops=0, bytes_accessed=2 * 1024 * 1024, transcendentals=0),
        name="assemble",
    )(*me[1:], *[in_vmem(x) for x in held.values()])
    *late, _, _ = lax.optimization_barrier((*late, token, histories[2][3]))
    late = {(1, 2): late, (1, 3): [over_core(x) for x in late]}

    rows = norb // hist_size
    ring = ring_of(hist_size) if hist_size <= 8 else []
    arrived, own, firsts = [], [], []
    for chunk, each in enumerate(sizes):
        if ring:
            out_shape = [pltpu.VMEM((2, each, rows, width), jnp.float32)] * hist_size
        else:
            out_shape = [pltpu.VMEM((2, each, norb, width), jnp.float32)]
        count, aliases, masks = len(out_shape), {}, ()
        after = lax.optimization_barrier((me[0], firsts[chunk - 2]))[0] if chunk >= 2 and ring else me[0]
        operands = [after, *me[1:]] + [in_vmem(x) for x in histories[chunk][:3]] + [in_vmem(x) for x in left]
        if chunk == 0:
            masks = tuple(late)
            operands += [in_vmem(x) for pair in late.values() for x in pair]
            out_shape += [pltpu.VMEM(left_shape, jnp.bfloat16)] * 2
            aliases = {6: count, 7: count + 1}
        parts = pl.pallas_call(
            functools.partial(chunk_kernel, masks, ring),
            out_shape=out_shape,
            in_specs=[SMEM] * 3 + [VMEM] * (len(operands) - 3),
            out_specs=[VMEM] * len(out_shape),
            scratch_shapes=[pltpu.VMEM((each, hist_size, 2, rows, width), jnp.float32)],
            input_output_aliases=aliases,
            cost_estimate=pl.CostEstimate(
                flops=6 * each * slices * 2 * norb * norb * 2 * width, bytes_accessed=0, transcendentals=0
            ),
            compiler_params=limit(16),
            name=f"products_{chunk}",
        )(*operands)
        if chunk == 0:
            left, parts = parts[count:], parts[:count]
        if not ring:
            total = lax.psum_scatter(parts[0], "hist", scatter_dimension=2, tiled=True)
            arrived.append(total)
            own.append(jnp.zeros_like(total))
            continue
        pairs = [(ring[p], ring[(p + 1) % hist_size]) for p in range(hist_size)]
        moving = parts[0]
        for m in range(1, hist_size):
            moving = lax.ppermute(moving, "hist", pairs)
            if m == 1:
                firsts.append(moving)
            if m < hist_size - 1:
                moving = moving + parts[m]
        arrived.append(moving)
        own.append(parts[-1])
    return pl.pallas_call(
        step_kernel,
        out_shape=jax.ShapeDtypeStruct(current_row.shape, jnp.float32),
        in_specs=[VMEM] * (3 * chunks),
        out_specs=HBM,
        scratch_shapes=[pltpu.VMEM(current_row.shape, jnp.float32), pltpu.SemaphoreType.DMA((chunks,))],
        compiler_params=limit(4),
        name="step",
    )(*[in_vmem(x) for x in arrived + own + [h[3] for h in histories]])


def solution(mesh):
    in_specs = (
        P(None, "hist", "ocol", "orow"),
        P(None, "hist", "orow", "ocol"),
        P(None, "hist", "ocol", None, "orow"),
        P(None, "ocol", "hist", "orow"),
        P("hist", None),
        P("hist"),
        P(),
    )
    out_specs = P(None, "ocol", "hist", "orow")
    body = functools.partial(on_device, mesh.shape["hist"], mesh.shape["orow"], mesh.shape["ocol"])
    return jax.shard_map(
        body, mesh=mesh, in_specs=in_specs, out_specs=out_specs, check_vma=False
    )
```

```python
import functools

import jax
import jax.numpy as jnp
from jax import lax
from jax.experimental import pallas as pl
from jax.experimental.pallas import tpu as pltpu
from jax.sharding import PartitionSpec as P

coupling_square = 0.25
hopping = 4.0
time_step = 0.01
VMEM = pl.BlockSpec(memory_space=pltpu.VMEM)
SMEM = pl.BlockSpec(memory_space=pltpu.SMEM)
HBM = pl.BlockSpec(memory_space=pltpu.HBM)


def sigma_kernel(hist_ref, orow_ref, ocol_ref, step_ref, table_hbm, lesser_hbm, greater_hbm, out_ref, lesser, greater, table_ref, sems):
    slices = lesser.shape[1]
    copies = [
        pltpu.make_async_copy(source, target, sems.at[place])
        for place, (source, target) in enumerate(
            [(table_hbm, table_ref), (lesser_hbm, lesser), (greater_hbm, greater)]
        )
    ]
    for copy in copies:
        copy.start()
    for copy in copies:
        copy.wait()
    for s in range(slices):
        numerator = jnp.full((1, lesser.shape[3]), table_ref[s], jnp.int32).astype(jnp.float32)
        weight = jnp.where(hist_ref[0] * slices + s <= step_ref[0], numerator / 24.0, 0.0)
        a_re, a_im = lesser[0, s], lesser[1, s]
        b_re, b_im = greater[0, s], greater[1, s]
        square_re = a_re * a_re - a_im * a_im
        square_im = 2.0 * a_re * a_im
        scale = coupling_square * weight
        out_ref[0, s] = scale * (square_re * b_re - square_im * b_im)
        out_ref[1, s] = scale * (square_re * b_im + square_im * b_re)


def split(x):
    high = x.astype(jnp.bfloat16)
    return high, (x - high.astype(jnp.float32)).astype(jnp.bfloat16)


def history_kernel(
    first, advanced_hbm, row_hbm, adjacency_hbm, high_ref, low_ref, hop_ref, row, advanced, adjacency, sems
):
    slices, each, width = advanced.shape[1], advanced.shape[2], advanced.shape[4]
    near = [
        pltpu.make_async_copy(row_hbm.at[:, pl.ds(first, each)], row, sems.at[each]),
        pltpu.make_async_copy(adjacency_hbm, adjacency, sems.at[each + 1]),
    ]
    far = [
        pltpu.make_async_copy(advanced_hbm.at[:, :, first + t], advanced.at[:, :, t], sems.at[t]) for t in range(each)
    ]
    for copy in near + far:
        copy.start()
    for copy in near:
        copy.wait()
    graph = (-hopping * adjacency[...].astype(jnp.float32)).T.astype(jnp.bfloat16)
    for t in range(each):
        place = t * 2 * width
        row_high, row_low = split(jnp.concatenate([row[0, t], row[1, t]], axis=1))
        hop_ref[:, place : place + 2 * width] = jnp.dot(
            graph, row_high, preferred_element_type=jnp.float32
        ) + jnp.dot(graph, row_low, preferred_element_type=jnp.float32)
    for t in range(each):
        far[t].wait()
        for s in range(slices):
            for part in range(2):
                place = (2 * t + part) * width
                high, low = split(advanced[part, s, t])
                high_ref[s, :, place : place + width] = high
                low_ref[s, :, place : place + width] = low


def assemble(masks, my_orow, my_ocol, blocks, left_high, left_low):
    for (flip_orow, flip_ocol), block in zip(masks, blocks):
        at_orow = jnp.bitwise_xor(my_orow, flip_orow)
        at_ocol = jnp.bitwise_xor(my_ocol, flip_ocol)
        for s in range(left_high.shape[0]):
            for part in range(2):
                high, low = split(block(part, s) if callable(block) else block[part, s])
                left_high[s, at_orow, part, at_ocol] = high
                left_low[s, at_orow, part, at_ocol] = low


def assemble_kernel(masks, orow_ref, ocol_ref, *refs):
    assemble(masks, orow_ref[0], ocol_ref[0], refs[:-3], refs[-3], refs[-2])
    refs[-1][...] = jnp.zeros_like(refs[-1])


def halves_kernel(first_ref, second_ref, first_half, second_half):
    slices = first_half.shape[1]
    first_half[...] = first_ref[:, :slices]
    second_half[...] = second_ref[:, slices:]


def join(halves):
    half = halves[0].shape[1]
    return lambda part, s: halves[s // half][part, s % half]


def chunk_kernel(masks, ring, hist_ref, orow_ref, ocol_ref, right_high, right_low, hop_ref, left_high, left_low, *refs):
    outs, result = refs[2 * len(masks) : -1], refs[-1]
    if masks:
        left_high, left_low, outs = outs[-2], outs[-1], outs[:-2]
        blocks = [join(refs[2 * place : 2 * place + 2]) for place in range(len(masks))]
        assemble(masks, orow_ref[0], ocol_ref[0], blocks, left_high, left_low)
    slices, halves = left_high.shape[:2]
    norb = right_high.shape[1]
    width = outs[0].shape[3]

    def left(ref, s):
        return jnp.concatenate([ref[s, half].reshape(2 * norb, norb // halves) for half in range(halves)], axis=1)

    total = None
    for s in range(slices):
        high = right_high[s]
        here = jnp.dot(
            jnp.concatenate([left(left_high, s), left(left_high, s), left(left_low, s)], axis=1),
            jnp.concatenate([high, right_low[s], high], axis=0),
            preferred_element_type=jnp.float32,
        )
        total = here if total is None else total + here
    for t in range(outs[0].shape[1]):
        at = 2 * width * t
        sum_re = total[:norb, at : at + width] - total[norb:, at + width : at + 2 * width] + hop_ref[:, at : at + width]
        sum_im = total[:norb, at + width : at + 2 * width] + total[norb:, at : at + width] + hop_ref[:, at + width : at + 2 * width]
        if not ring:
            outs[0][0, t] = sum_re
            outs[0][1, t] = sum_im
            continue
        rows = norb // len(ring)
        for block in range(len(ring)):
            result[t, block, 0] = sum_re[block * rows : (block + 1) * rows]
            result[t, block, 1] = sum_im[block * rows : (block + 1) * rows]
    if not ring:
        return
    size = len(ring)
    my_hist = hist_ref[0]
    my_place = sum(jnp.where(my_hist == h, ring.index(h), 0) for h in range(size))
    for step, out in enumerate(outs):
        place = my_place + (size - 1 - step)
        place = jnp.where(place >= size, place - size, place)
        block = sum(jnp.where(place == p, ring[p], 0) for p in range(size))
        for t in range(out.shape[1]):
            out[0, t] = result[t, block, 0]
            out[1, t] = result[t, block, 1]


def step_kernel(*refs):
    chunks = (len(refs) - 3) // 3
    arrived, own, row = refs[:chunks], refs[chunks : 2 * chunks], refs[2 * chunks : 3 * chunks]
    out_hbm, out, sems = refs[3 * chunks :]
    copies, first = [], 0
    for chunk in range(chunks):
        here = pl.ds(first, own[chunk].shape[1])
        first += own[chunk].shape[1]
        out[0, here] = row[chunk][0] + time_step * (arrived[chunk][1] + own[chunk][1])
        out[1, here] = row[chunk][1] - time_step * (arrived[chunk][0] + own[chunk][0])
        copies.append(pltpu.make_async_copy(out.at[:, here], out_hbm.at[:, here], sems.at[chunk]))
        copies[-1].start()
    for copy in copies:
        copy.wait()


def ring_of(size):
    return [place for place in range(size) if place == 0 or place % 2 == 1] + [
        place for place in range(size - 1, 0, -1) if place % 2 == 0
    ]


def limit(mebibytes):
    return pltpu.CompilerParams(vmem_limit_bytes=mebibytes * 1024 * 1024)


def in_vmem(x):
    return pltpu.with_memory_space_constraint(x, pltpu.VMEM)


def in_hbm(x):
    return pltpu.with_memory_space_constraint(x, pltpu.HBM)


def add_kernel(left_ref, right_ref, out_ref):
    out_ref[...] = left_ref[...] + right_ref[...]


def add(left, right):
    return pl.pallas_call(
        add_kernel,
        out_shape=pltpu.VMEM(left.shape, left.dtype),
        in_specs=[VMEM] * 2,
        out_specs=VMEM,
        compiler_params=limit(4),
        name="add",
    )(in_vmem(left), in_vmem(right))


def on_device(
    hist_size, orow_size, ocol_size, lesser_hist, greater_hist, advanced_hist, current_row, adjacency, weight_table, step_index
):
    slices, times, norb, width = advanced_hist.shape[1:]
    block = lesser_hist.shape
    my_hist, my_orow, my_ocol = lax.axis_index("hist"), lax.axis_index("orow"), lax.axis_index("ocol")
    me = [index.reshape(1).astype(jnp.int32) for index in (my_hist, my_orow, my_ocol)]
    sigma = pl.pallas_call(
        sigma_kernel,
        out_shape=pltpu.VMEM(block, jnp.float32),
        in_specs=[SMEM] * 4 + [HBM] * 3,
        out_specs=VMEM,
        scratch_shapes=[
            pltpu.VMEM(block, jnp.float32),
            pltpu.VMEM(block, jnp.float32),
            pltpu.SMEM(weight_table.shape, jnp.int32),
            pltpu.SemaphoreType.DMA((3,)),
        ],
        compiler_params=limit(4),
        name="sigma",
    )(*me, step_index, in_hbm(weight_table), in_hbm(lesser_hist), in_hbm(jnp.swapaxes(greater_hist, 2, 3)))

    short = times // 4
    sizes = [short, (times - short) // 2, times - short - (times - short) // 2]
    chunks = len(sizes)

    def history(chunk):
        each = sizes[chunk]
        return list(pl.pallas_call(
            functools.partial(history_kernel, sum(sizes[:chunk])),
            out_shape=[
                pltpu.VMEM((slices, norb, each * 2 * width), jnp.bfloat16),
                pltpu.VMEM((slices, norb, each * 2 * width), jnp.bfloat16),
                pltpu.VMEM((norb, each * 2 * width), jnp.float32),
                pltpu.VMEM((2, each) + current_row.shape[2:], jnp.float32),
            ],
            in_specs=[HBM] * 3,
            out_specs=[VMEM] * 4,
            scratch_shapes=[
                pltpu.VMEM((2, slices, each, norb, width), jnp.float32),
                pltpu.VMEM(adjacency.shape, jnp.int32),
                pltpu.SemaphoreType.DMA((each + 2,)),
            ],
            compiler_params=limit(12),
            cost_estimate=pl.CostEstimate(flops=0, bytes_accessed=4 * 1024 * 1024, transcendentals=0),
            name=f"history_{chunk}",
        )(in_hbm(advanced_hist), in_hbm(current_row), in_hbm(adjacency)))

    def moved(x, target):
        pairs = [
            (r * ocol_size + c, target(r, c)[0] * ocol_size + target(r, c)[1])
            for r in range(orow_size)
            for c in range(ocol_size)
        ]
        return lax.ppermute(x, ("orow", "ocol"), pairs)

    def over_core(x):
        return moved(x, lambda r, c: (r, c ^ 1))

    histories = [history(chunk) for chunk in range(chunks)]
    held = {(0, 0): sigma}
    held[(1, 0)] = moved(sigma, lambda r, c: (r ^ 1, c))
    held[(0, 2)] = moved(sigma, lambda r, c: (r, c ^ 2))
    held[(0, 1)] = over_core(sigma)
    over_orow, over_ocol, *_ = lax.optimization_barrier(
        (held[(1, 0)], held[(0, 2)], histories[0][3], histories[1][3])
    )
    half_shape = (2, slices // 2) + block[2:]
    halves = pl.pallas_call(
        halves_kernel,
        out_shape=[pltpu.VMEM(half_shape, jnp.float32), pltpu.VMEM((2, slices - slices // 2) + block[2:], jnp.float32)],
        in_specs=[VMEM] * 2,
        out_specs=[VMEM] * 2,
        compiler_params=limit(4),
        name="halves",
    )(in_vmem(over_orow), in_vmem(over_ocol))
    late = (moved(halves[0], lambda r, c: (r, c ^ 2)), moved(halves[1], lambda r, c: (r ^ 1, c)))
    held[(1, 1)] = over_core(held[(1, 0)])
    held[(0, 3)] = over_core(held[(0, 2)])
    left_shape = (slices, orow_size, 2, ocol_size) + block[2:]
    *left, token = pl.pallas_call(
        functools.partial(assemble_kernel, tuple(held)),
        out_shape=[pltpu.VMEM(left_shape, jnp.bfloat16)] * 2 + [pltpu.VMEM((8, 128), jnp.float32)],
        in_specs=[SMEM] * 2 + [VMEM] * len(held),
        out_specs=[VMEM] * 3,
        compiler_params=limit(4),
        cost_estimate=pl.CostEstimate(flops=0, bytes_accessed=2 * 1024 * 1024, transcendentals=0),
        name="assemble",
    )(*me[1:], *[in_vmem(x) for x in held.values()])
    *late, _, _ = lax.optimization_barrier((*late, token, histories[2][3]))
    late = {(1, 2): late, (1, 3): [over_core(x) for x in late]}

    rows = norb // hist_size
    ring = ring_of(hist_size) if hist_size <= 8 else []
    arrived, own, firsts = [], [], []
    for chunk, each in enumerate(sizes):
        if ring:
            out_shape = [pltpu.VMEM((2, each, rows, width), jnp.float32)] * hist_size
        else:
            out_shape = [pltpu.VMEM((2, each, norb, width), jnp.float32)]
        count, aliases, masks = len(out_shape), {}, ()
        after = lax.optimization_barrier((me[0], firsts[chunk - 2]))[0] if chunk >= 2 and ring else me[0]
        operands = [after, *me[1:]] + [in_vmem(x) for x in histories[chunk][:3]] + [in_vmem(x) for x in left]
        if chunk == 0:
            masks = tuple(late)
            operands += [in_vmem(x) for pair in late.values() for x in pair]
            out_shape += [pltpu.VMEM(left_shape, jnp.bfloat16)] * 2
            aliases = {6: count, 7: count + 1}
        parts = pl.pallas_call(
            functools.partial(chunk_kernel, masks, ring),
            out_shape=out_shape,
            in_specs=[SMEM] * 3 + [VMEM] * (len(operands) - 3),
            out_specs=[VMEM] * len(out_shape),
            scratch_shapes=[pltpu.VMEM((each, hist_size, 2, rows, width), jnp.float32)],
            input_output_aliases=aliases,
            cost_estimate=pl.CostEstimate(
                flops=6 * each * slices * 2 * norb * norb * 2 * width, bytes_accessed=0, transcendentals=0
            ),
            compiler_params=limit(16),
            name=f"products_{chunk}",
        )(*operands)
        if chunk == 0:
            left, parts = parts[count:], parts[:count]
        if not ring:
            total = lax.psum_scatter(parts[0], "hist", scatter_dimension=2, tiled=True)
            arrived.append(total)
            own.append(jnp.zeros_like(total))
            continue
        pairs = [(ring[p], ring[(p + 1) % hist_size]) for p in range(hist_size)]
        moving = parts[0]
        for m in range(1, hist_size):
            moving = lax.ppermute(moving, "hist", pairs)
            if m == 1:
                firsts.append(moving)
            if m < hist_size - 1:
                moving = add(moving, parts[m])
        arrived.append(moving)
        own.append(parts[-1])
    return pl.pallas_call(
        step_kernel,
        out_shape=jax.ShapeDtypeStruct(current_row.shape, jnp.float32),
        in_specs=[VMEM] * (3 * chunks),
        out_specs=HBM,
        scratch_shapes=[pltpu.VMEM(current_row.shape, jnp.float32), pltpu.SemaphoreType.DMA((chunks,))],
        compiler_params=limit(4),
        name="step",
    )(*[in_vmem(x) for x in arrived + own + [h[3] for h in histories]])


def solution(mesh):
    in_specs = (
        P(None, "hist", "ocol", "orow"),
        P(None, "hist", "orow", "ocol"),
        P(None, "hist", "ocol", None, "orow"),
        P(None, "ocol", "hist", "orow"),
        P("hist", None),
        P("hist"),
        P(),
    )
    out_specs = P(None, "ocol", "hist", "orow")
    body = functools.partial(on_device, mesh.shape["hist"], mesh.shape["orow"], mesh.shape["ocol"])
    return jax.shard_map(
        body, mesh=mesh, in_specs=in_specs, out_specs=out_specs, check_vma=False
    )
```

```python
import functools

import jax
import jax.numpy as jnp
from jax import lax
from jax.experimental import pallas as pl
from jax.experimental.pallas import tpu as pltpu
from jax.sharding import PartitionSpec as P

coupling_square = 0.25
hopping = 4.0
time_step = 0.01
VMEM = pl.BlockSpec(memory_space=pltpu.VMEM)
SMEM = pl.BlockSpec(memory_space=pltpu.SMEM)
HBM = pl.BlockSpec(memory_space=pltpu.HBM)


def sigma_kernel(hist_ref, orow_ref, ocol_ref, step_ref, table_hbm, lesser_hbm, greater_hbm, out_ref, early_ref, late_ref, lesser, greater, table_ref, sems):
    slices = lesser.shape[1]
    copies = [
        pltpu.make_async_copy(source, target, sems.at[place])
        for place, (source, target) in enumerate(
            [(table_hbm, table_ref), (lesser_hbm, lesser), (greater_hbm, greater)]
        )
    ]
    for copy in copies:
        copy.start()
    for copy in copies:
        copy.wait()
    for s in range(slices):
        numerator = jnp.full((1, lesser.shape[3]), table_ref[s], jnp.int32).astype(jnp.float32)
        weight = jnp.where(hist_ref[0] * slices + s <= step_ref[0], numerator / 24.0, 0.0)
        a_re, a_im = lesser[0, s], lesser[1, s]
        b_re, b_im = greater[0, s], greater[1, s]
        square_re = a_re * a_re - a_im * a_im
        square_im = 2.0 * a_re * a_im
        scale = coupling_square * weight
        half = early_ref.shape[1]
        part_ref = early_ref if s < half else late_ref
        for part, value in enumerate((square_re * b_re - square_im * b_im, square_re * b_im + square_im * b_re)):
            out_ref[part, s] = scale * value
            part_ref[part, s % half] = scale * value


def split(x):
    high = x.astype(jnp.bfloat16)
    return high, (x - high.astype(jnp.float32)).astype(jnp.bfloat16)


def history_kernel(
    first, order_ref, advanced_hbm, row_hbm, adjacency_hbm, high_ref, low_ref, hop_ref, row, advanced, adjacency, sems
):
    slices, each, width = advanced.shape[1], advanced.shape[2], advanced.shape[4]
    near = [
        pltpu.make_async_copy(row_hbm.at[:, pl.ds(first, each)], row, sems.at[each]),
        pltpu.make_async_copy(adjacency_hbm, adjacency, sems.at[each + 1]),
    ]
    far = [
        pltpu.make_async_copy(advanced_hbm.at[:, :, first + t], advanced.at[:, :, t], sems.at[t]) for t in range(each)
    ]
    for copy in near + far:
        copy.start()
    for copy in near:
        copy.wait()
    graph = (-hopping * adjacency[...].astype(jnp.float32)).T.astype(jnp.bfloat16)
    for t in range(each):
        place = t * 2 * width
        row_high, row_low = split(jnp.concatenate([row[0, t], row[1, t]], axis=1))
        hop_ref[:, place : place + 2 * width] = jnp.dot(
            graph, row_high, preferred_element_type=jnp.float32
        ) + jnp.dot(graph, row_low, preferred_element_type=jnp.float32)
    for t in range(each):
        far[t].wait()
        for s in range(slices):
            for part in range(2):
                place = (2 * t + part) * width
                high, low = split(advanced[part, s, t])
                high_ref[s, :, place : place + width] = high
                low_ref[s, :, place : place + width] = low


def assemble(masks, my_orow, my_ocol, blocks, left_high, left_low):
    for (flip_orow, flip_ocol), block in zip(masks, blocks):
        at_orow = jnp.bitwise_xor(my_orow, flip_orow)
        at_ocol = jnp.bitwise_xor(my_ocol, flip_ocol)
        for s in range(left_high.shape[0]):
            for part in range(2):
                high, low = split(block(part, s) if callable(block) else block[part, s])
                left_high[s, at_orow, part, at_ocol] = high
                left_low[s, at_orow, part, at_ocol] = low


def assemble_kernel(masks, orow_ref, ocol_ref, own, own_partner, both, both_partner, left_high, left_low, token):
    blocks = [own, own_partner, both.at[0], both.at[1], both_partner.at[0], both_partner.at[1]]
    assemble(masks, orow_ref[0], ocol_ref[0], blocks, left_high, left_low)
    token[...] = jnp.zeros_like(token)


def collect_kernel(a_early, a_late, b_early, b_late, out_ref):
    half = a_early.shape[1]
    for place, (early, late) in enumerate(((a_early, a_late), (b_early, b_late))):
        out_ref[place, :, :half] = early[...]
        out_ref[place, :, half:] = late[...]


def join(halves):
    half = halves[0].shape[1]
    return lambda part, s: halves[s // half][part, s % half]


def chunk_kernel(masks, ring, hist_ref, orow_ref, ocol_ref, right_high, right_low, hop_ref, left_high, left_low, *refs):
    outs, result = refs[2 * len(masks) : -1], refs[-1]
    if masks:
        left_high, left_low, outs = outs[-2], outs[-1], outs[:-2]
        blocks = [join(refs[2 * place : 2 * place + 2]) for place in range(len(masks))]
        assemble(masks, orow_ref[0], ocol_ref[0], blocks, left_high, left_low)
    slices, halves = left_high.shape[:2]
    norb = right_high.shape[1]
    width = outs[0].shape[3]

    def left(ref, s):
        return jnp.concatenate([ref[s, half].reshape(2 * norb, norb // halves) for half in range(halves)], axis=1)

    total = None
    for s in range(slices):
        high = right_high[s]
        here = jnp.dot(
            jnp.concatenate([left(left_high, s), left(left_high, s), left(left_low, s)], axis=1),
            jnp.concatenate([high, right_low[s], high], axis=0),
            preferred_element_type=jnp.float32,
        )
        total = here if total is None else total + here
    for t in range(outs[0].shape[1]):
        at = 2 * width * t
        sum_re = total[:norb, at : at + width] - total[norb:, at + width : at + 2 * width] + hop_ref[:, at : at + width]
        sum_im = total[:norb, at + width : at + 2 * width] + total[norb:, at : at + width] + hop_ref[:, at + width : at + 2 * width]
        if not ring:
            outs[0][0, t] = sum_re
            outs[0][1, t] = sum_im
            continue
        rows = norb // len(ring)
        for block in range(len(ring)):
            result[t, block, 0] = sum_re[block * rows : (block + 1) * rows]
            result[t, block, 1] = sum_im[block * rows : (block + 1) * rows]
    if not ring:
        return
    size = len(ring)
    my_hist = hist_ref[0]
    my_place = sum(jnp.where(my_hist == h, ring.index(h), 0) for h in range(size))
    for step, out in enumerate(outs):
        place = my_place + (size - 1 - step)
        place = jnp.where(place >= size, place - size, place)
        block = sum(jnp.where(place == p, ring[p], 0) for p in range(size))
        for t in range(out.shape[1]):
            out[0, t] = result[t, block, 0]
            out[1, t] = result[t, block, 1]


def step_kernel(*refs):
    chunks = (len(refs) - 3) // 3
    arrived, own, row = refs[:chunks], refs[chunks : 2 * chunks], refs[2 * chunks : 3 * chunks]
    out_hbm, out, sems = refs[3 * chunks :]
    copies, first = [], 0
    for chunk in range(chunks):
        here = pl.ds(first, own[chunk].shape[1])
        first += own[chunk].shape[1]
        out[0, here] = row[chunk][0] + time_step * (arrived[chunk][1] + own[chunk][1])
        out[1, here] = row[chunk][1] - time_step * (arrived[chunk][0] + own[chunk][0])
        copies.append(pltpu.make_async_copy(out.at[:, here], out_hbm.at[:, here], sems.at[chunk]))
        copies[-1].start()
    for copy in copies:
        copy.wait()


def ring_of(size):
    return [place for place in range(size) if place == 0 or place % 2 == 1] + [
        place for place in range(size - 1, 0, -1) if place % 2 == 0
    ]


def limit(mebibytes):
    return pltpu.CompilerParams(vmem_limit_bytes=mebibytes * 1024 * 1024)


def in_vmem(x):
    return pltpu.with_memory_space_constraint(x, pltpu.VMEM)


def in_hbm(x):
    return pltpu.with_memory_space_constraint(x, pltpu.HBM)


def add_kernel(left_ref, right_ref, out_ref):
    out_ref[...] = left_ref[...] + right_ref[...]


def add(left, right):
    return pl.pallas_call(
        add_kernel,
        out_shape=pltpu.VMEM(left.shape, left.dtype),
        in_specs=[VMEM] * 2,
        out_specs=VMEM,
        compiler_params=limit(4),
        name="add",
    )(in_vmem(left), in_vmem(right))


def on_device(
    hist_size, orow_size, ocol_size, lesser_hist, greater_hist, advanced_hist, current_row, adjacency, weight_table, step_index
):
    slices, times, norb, width = advanced_hist.shape[1:]
    block = lesser_hist.shape
    my_hist, my_orow, my_ocol = lax.axis_index("hist"), lax.axis_index("orow"), lax.axis_index("ocol")
    me = [index.reshape(1).astype(jnp.int32) for index in (my_hist, my_orow, my_ocol)]
    half_shape = (2, slices // 2) + block[2:]
    sigma, early, late = pl.pallas_call(
        sigma_kernel,
        out_shape=[pltpu.VMEM(shape, jnp.float32) for shape in (block, half_shape, half_shape)],
        in_specs=[SMEM] * 4 + [HBM] * 3,
        out_specs=[VMEM] * 3,
        scratch_shapes=[
            pltpu.VMEM(block, jnp.float32),
            pltpu.VMEM(block, jnp.float32),
            pltpu.SMEM(weight_table.shape, jnp.int32),
            pltpu.SemaphoreType.DMA((3,)),
        ],
        compiler_params=limit(4),
        name="sigma",
    )(*me, step_index, in_hbm(weight_table), in_hbm(lesser_hist), in_hbm(jnp.swapaxes(greater_hist, 2, 3)))

    short = times // 4
    sizes = [(times - short) // 2, times - short - (times - short) // 2, short]
    chunks = len(sizes)

    def history(chunk, order):
        each = sizes[chunk]
        return list(pl.pallas_call(
            functools.partial(history_kernel, sum(sizes[:chunk])),
            out_shape=[
                pltpu.VMEM((slices, norb, each * 2 * width), jnp.bfloat16),
                pltpu.VMEM((slices, norb, each * 2 * width), jnp.bfloat16),
                pltpu.VMEM((norb, each * 2 * width), jnp.float32),
                pltpu.VMEM((2, each) + current_row.shape[2:], jnp.float32),
            ],
            in_specs=[SMEM] + [HBM] * 3,
            out_specs=[VMEM] * 4,
            scratch_shapes=[
                pltpu.VMEM((2, slices, each, norb, width), jnp.float32),
                pltpu.VMEM(adjacency.shape, jnp.int32),
                pltpu.SemaphoreType.DMA((each + 2,)),
            ],
            compiler_params=limit(12),
            cost_estimate=pl.CostEstimate(flops=0, bytes_accessed=4 * 1024 * 1024, transcendentals=0),
            name=f"history_{chunk}",
        )(order, in_hbm(advanced_hist), in_hbm(current_row), in_hbm(adjacency)))

    def moved(x, target):
        pairs = [
            (r * ocol_size + c, target(r, c)[0] * ocol_size + target(r, c)[1])
            for r in range(orow_size)
            for c in range(ocol_size)
        ]
        return lax.ppermute(x, ("orow", "ocol"), pairs)

    def over_core(x):
        return moved(x, lambda r, c: (r, c ^ 1))

    def over_orow(x):
        return moved(x, lambda r, c: (r ^ 1, c))

    def over_ocol(x):
        return moved(x, lambda r, c: (r, c ^ 2))

    orow_early, ocol_late, orow_late, ocol_early = over_orow(early), over_ocol(late), over_orow(late), over_ocol(early)
    own_partner = over_core(sigma)
    histories = [history(0, me[0])]
    far_early, far_late, _ = lax.optimization_barrier((orow_early, ocol_late, histories[0][3]))
    far = [over_ocol(far_early), over_orow(far_late)]
    order = lax.optimization_barrier((me[0], far_early, histories[0][3]))[0]
    histories += [history(chunk, order) for chunk in range(1, chunks)]
    orow_late, ocol_early, _ = lax.optimization_barrier((orow_late, ocol_early, histories[1][3]))
    both = pl.pallas_call(
        collect_kernel,
        out_shape=pltpu.VMEM((2,) + block, jnp.float32),
        in_specs=[VMEM] * 4,
        out_specs=VMEM,
        compiler_params=limit(4),
        name="collect",
    )(*[in_vmem(x) for x in (orow_early, orow_late, ocol_early, ocol_late)])
    both_partner = over_core(both)
    left_shape = (slices, orow_size, 2, ocol_size) + block[2:]
    *left, token = pl.pallas_call(
        functools.partial(assemble_kernel, ((0, 0), (0, 1), (1, 0), (0, 2), (1, 1), (0, 3))),
        out_shape=[pltpu.VMEM(left_shape, jnp.bfloat16)] * 2 + [pltpu.VMEM((8, 128), jnp.float32)],
        in_specs=[SMEM] * 2 + [VMEM] * 4,
        out_specs=[VMEM] * 3,
        compiler_params=limit(4),
        cost_estimate=pl.CostEstimate(flops=0, bytes_accessed=2 * 1024 * 1024, transcendentals=0),
        name="assemble",
    )(*me[1:], *[in_vmem(x) for x in (sigma, own_partner, both, both_partner)])
    *far, _, _ = lax.optimization_barrier((*far, *[h[3] for h in histories[1:]]))
    far_partner = [over_core(x) for x in far]
    late = {(1, 2): far, (1, 3): far_partner}

    rows = norb // hist_size
    ring = ring_of(hist_size) if hist_size <= 8 else []
    arrived, own, firsts = [], [], []
    for chunk, each in enumerate(sizes):
        if ring:
            out_shape = [pltpu.VMEM((2, each, rows, width), jnp.float32)] * hist_size
        else:
            out_shape = [pltpu.VMEM((2, each, norb, width), jnp.float32)]
        count, aliases, masks = len(out_shape), {}, ()
        after = lax.optimization_barrier((me[0], firsts[chunk - 2]))[0] if chunk >= 2 and ring else me[0]
        operands = [after, *me[1:]] + [in_vmem(x) for x in histories[chunk][:3]] + [in_vmem(x) for x in left]
        if chunk == 0:
            masks = tuple(late)
            operands += [in_vmem(x) for pair in late.values() for x in pair]
            out_shape += [pltpu.VMEM(left_shape, jnp.bfloat16)] * 2
            aliases = {6: count, 7: count + 1}
        parts = pl.pallas_call(
            functools.partial(chunk_kernel, masks, ring),
            out_shape=out_shape,
            in_specs=[SMEM] * 3 + [VMEM] * (len(operands) - 3),
            out_specs=[VMEM] * len(out_shape),
            scratch_shapes=[pltpu.VMEM((each, hist_size, 2, rows, width), jnp.float32)],
            input_output_aliases=aliases,
            cost_estimate=pl.CostEstimate(
                flops=6 * each * slices * 2 * norb * norb * 2 * width, bytes_accessed=0, transcendentals=0
            ),
            compiler_params=limit(16),
            name=f"products_{chunk}",
        )(*operands)
        if chunk == 0:
            left, parts = parts[count:], parts[:count]
        if not ring:
            total = lax.psum_scatter(parts[0], "hist", scatter_dimension=2, tiled=True)
            arrived.append(total)
            own.append(jnp.zeros_like(total))
            continue
        pairs = [(ring[p], ring[(p + 1) % hist_size]) for p in range(hist_size)]
        moving = parts[0]
        for m in range(1, hist_size):
            moving = lax.ppermute(moving, "hist", pairs)
            if m == 1:
                firsts.append(moving)
            if m < hist_size - 1:
                moving = add(moving, parts[m])
        arrived.append(moving)
        own.append(parts[-1])
    return pl.pallas_call(
        step_kernel,
        out_shape=jax.ShapeDtypeStruct(current_row.shape, jnp.float32),
        in_specs=[VMEM] * (3 * chunks),
        out_specs=HBM,
        scratch_shapes=[pltpu.VMEM(current_row.shape, jnp.float32), pltpu.SemaphoreType.DMA((chunks,))],
        compiler_params=limit(4),
        name="step",
    )(*[in_vmem(x) for x in arrived + own + [h[3] for h in histories]])


def solution(mesh):
    in_specs = (
        P(None, "hist", "ocol", "orow"),
        P(None, "hist", "orow", "ocol"),
        P(None, "hist", "ocol", None, "orow"),
        P(None, "ocol", "hist", "orow"),
        P("hist", None),
        P("hist"),
        P(),
    )
    out_specs = P(None, "ocol", "hist", "orow")
    body = functools.partial(on_device, mesh.shape["hist"], mesh.shape["orow"], mesh.shape["ocol"])
    return jax.shard_map(
        body, mesh=mesh, in_specs=in_specs, out_specs=out_specs, check_vma=False
    )
```

```python
import functools

import jax
import jax.numpy as jnp
from jax import lax
from jax.experimental import pallas as pl
from jax.experimental.pallas import tpu as pltpu
from jax.sharding import PartitionSpec as P

coupling_square = 0.25
hopping = 4.0
time_step = 0.01
VMEM = pl.BlockSpec(memory_space=pltpu.VMEM)
SMEM = pl.BlockSpec(memory_space=pltpu.SMEM)
HBM = pl.BlockSpec(memory_space=pltpu.HBM)


def sigma_kernel(hist_ref, orow_ref, ocol_ref, step_ref, table_hbm, lesser_hbm, greater_hbm, out_ref, early_ref, late_ref, lesser, greater, table_ref, sems):
    slices = lesser.shape[1]
    copies = [
        pltpu.make_async_copy(source, target, sems.at[place])
        for place, (source, target) in enumerate(
            [(table_hbm, table_ref), (lesser_hbm, lesser), (greater_hbm, greater)]
        )
    ]
    for copy in copies:
        copy.start()
    for copy in copies:
        copy.wait()
    for s in range(slices):
        numerator = jnp.full((1, lesser.shape[3]), table_ref[s], jnp.int32).astype(jnp.float32)
        weight = jnp.where(hist_ref[0] * slices + s <= step_ref[0], numerator / 24.0, 0.0)
        a_re, a_im = lesser[0, s], lesser[1, s]
        b_re, b_im = greater[0, s], greater[1, s]
        square_re = a_re * a_re - a_im * a_im
        square_im = 2.0 * a_re * a_im
        scale = coupling_square * weight
        half = early_ref.shape[1]
        part_ref = early_ref if s < half else late_ref
        for part, value in enumerate((square_re * b_re - square_im * b_im, square_re * b_im + square_im * b_re)):
            out_ref[part, s] = scale * value
            part_ref[part, s % half] = scale * value


def split(x):
    high = x.astype(jnp.bfloat16)
    return high, (x - high.astype(jnp.float32)).astype(jnp.bfloat16)


def history_kernel(
    first, order_ref, advanced_hbm, row_hbm, adjacency_hbm, high_ref, low_ref, hop_ref, row, advanced, adjacency, sems
):
    slices, each, width = advanced.shape[1], advanced.shape[2], advanced.shape[4]
    near = [
        pltpu.make_async_copy(row_hbm.at[:, pl.ds(first, each)], row, sems.at[each]),
        pltpu.make_async_copy(adjacency_hbm, adjacency, sems.at[each + 1]),
    ]
    far = [
        pltpu.make_async_copy(advanced_hbm.at[:, :, first + t], advanced.at[:, :, t], sems.at[t]) for t in range(each)
    ]
    for copy in near + far:
        copy.start()
    for copy in near:
        copy.wait()
    graph = (-hopping * adjacency[...].astype(jnp.float32)).T.astype(jnp.bfloat16)
    for t in range(each):
        place = t * 2 * width
        row_high, row_low = split(jnp.concatenate([row[0, t], row[1, t]], axis=1))
        hop_ref[:, place : place + 2 * width] = jnp.dot(
            graph, row_high, preferred_element_type=jnp.float32
        ) + jnp.dot(graph, row_low, preferred_element_type=jnp.float32)
    for t in range(each):
        far[t].wait()
        for s in range(slices):
            for part in range(2):
                place = (2 * t + part) * width
                high, low = split(advanced[part, s, t])
                high_ref[s, :, place : place + width] = high
                low_ref[s, :, place : place + width] = low


def assemble(masks, my_orow, my_ocol, blocks, left_high, left_low):
    for (flip_orow, flip_ocol), block in zip(masks, blocks):
        at_orow = jnp.bitwise_xor(my_orow, flip_orow)
        at_ocol = jnp.bitwise_xor(my_ocol, flip_ocol)
        for s in range(left_high.shape[0]):
            for part in range(2):
                high, low = split(block(part, s) if callable(block) else block[part, s])
                left_high[s, at_orow, part, at_ocol] = high
                left_low[s, at_orow, part, at_ocol] = low


def assemble_kernel(masks, orow_ref, ocol_ref, own, own_partner, *refs):
    halves, (left_high, left_low, token) = refs[:-3], refs[-3:]
    blocks = [own, own_partner] + [join(halves[2 * place : 2 * place + 2]) for place in range(len(halves) // 2)]
    assemble(masks, orow_ref[0], ocol_ref[0], blocks, left_high, left_low)
    token[...] = jnp.zeros_like(token)


def join(halves):
    half = halves[0].shape[1]
    return lambda part, s: halves[s // half][part, s % half]


def chunk_kernel(masks, ring, hist_ref, orow_ref, ocol_ref, right_high, right_low, hop_ref, left_high, left_low, *refs):
    outs, result = refs[2 * len(masks) : -1], refs[-1]
    if masks:
        left_high, left_low, outs = outs[-2], outs[-1], outs[:-2]
        blocks = [join(refs[2 * place : 2 * place + 2]) for place in range(len(masks))]
        assemble(masks, orow_ref[0], ocol_ref[0], blocks, left_high, left_low)
    slices, halves = left_high.shape[:2]
    norb = right_high.shape[1]
    width = outs[0].shape[3]

    def left(ref, s):
        return jnp.concatenate([ref[s, half].reshape(2 * norb, norb // halves) for half in range(halves)], axis=1)

    total = None
    for s in range(slices):
        high = right_high[s]
        here = jnp.dot(
            jnp.concatenate([left(left_high, s), left(left_high, s), left(left_low, s)], axis=1),
            jnp.concatenate([high, right_low[s], high], axis=0),
            preferred_element_type=jnp.float32,
        )
        total = here if total is None else total + here
    for t in range(outs[0].shape[1]):
        at = 2 * width * t
        sum_re = total[:norb, at : at + width] - total[norb:, at + width : at + 2 * width] + hop_ref[:, at : at + width]
        sum_im = total[:norb, at + width : at + 2 * width] + total[norb:, at : at + width] + hop_ref[:, at + width : at + 2 * width]
        if not ring:
            outs[0][0, t] = sum_re
            outs[0][1, t] = sum_im
            continue
        rows = norb // len(ring)
        for block in range(len(ring)):
            result[t, block, 0] = sum_re[block * rows : (block + 1) * rows]
            result[t, block, 1] = sum_im[block * rows : (block + 1) * rows]
    if not ring:
        return
    size = len(ring)
    my_hist = hist_ref[0]
    my_place = sum(jnp.where(my_hist == h, ring.index(h), 0) for h in range(size))
    for step, out in enumerate(outs):
        place = my_place + (size - 1 - step)
        place = jnp.where(place >= size, place - size, place)
        block = sum(jnp.where(place == p, ring[p], 0) for p in range(size))
        for t in range(out.shape[1]):
            out[0, t] = result[t, block, 0]
            out[1, t] = result[t, block, 1]


def step_kernel(*refs):
    chunks = (len(refs) - 3) // 3
    arrived, own, row = refs[:chunks], refs[chunks : 2 * chunks], refs[2 * chunks : 3 * chunks]
    out_hbm, out, sems = refs[3 * chunks :]
    copies, first = [], 0
    for chunk in range(chunks):
        here = pl.ds(first, own[chunk].shape[1])
        first += own[chunk].shape[1]
        out[0, here] = row[chunk][0] + time_step * (arrived[chunk][1] + own[chunk][1])
        out[1, here] = row[chunk][1] - time_step * (arrived[chunk][0] + own[chunk][0])
        copies.append(pltpu.make_async_copy(out.at[:, here], out_hbm.at[:, here], sems.at[chunk]))
        copies[-1].start()
    for copy in copies:
        copy.wait()


def ring_of(size):
    return [place for place in range(size) if place == 0 or place % 2 == 1] + [
        place for place in range(size - 1, 0, -1) if place % 2 == 0
    ]


def limit(mebibytes):
    return pltpu.CompilerParams(vmem_limit_bytes=mebibytes * 1024 * 1024)


def in_vmem(x):
    return pltpu.with_memory_space_constraint(x, pltpu.VMEM)


def in_hbm(x):
    return pltpu.with_memory_space_constraint(x, pltpu.HBM)


def add_kernel(left_ref, right_ref, out_ref):
    out_ref[...] = left_ref[...] + right_ref[...]


def add(left, right):
    return pl.pallas_call(
        add_kernel,
        out_shape=pltpu.VMEM(left.shape, left.dtype),
        in_specs=[VMEM] * 2,
        out_specs=VMEM,
        compiler_params=limit(4),
        name="add",
    )(in_vmem(left), in_vmem(right))


def on_device(
    hist_size, orow_size, ocol_size, lesser_hist, greater_hist, advanced_hist, current_row, adjacency, weight_table, step_index
):
    slices, times, norb, width = advanced_hist.shape[1:]
    block = lesser_hist.shape
    my_hist, my_orow, my_ocol = lax.axis_index("hist"), lax.axis_index("orow"), lax.axis_index("ocol")
    me = [index.reshape(1).astype(jnp.int32) for index in (my_hist, my_orow, my_ocol)]
    half_shape = (2, slices // 2) + block[2:]
    sigma, early, late = pl.pallas_call(
        sigma_kernel,
        out_shape=[pltpu.VMEM(shape, jnp.float32) for shape in (block, half_shape, half_shape)],
        in_specs=[SMEM] * 4 + [HBM] * 3,
        out_specs=[VMEM] * 3,
        scratch_shapes=[
            pltpu.VMEM(block, jnp.float32),
            pltpu.VMEM(block, jnp.float32),
            pltpu.SMEM(weight_table.shape, jnp.int32),
            pltpu.SemaphoreType.DMA((3,)),
        ],
        compiler_params=limit(4),
        name="sigma",
    )(*me, step_index, in_hbm(weight_table), in_hbm(lesser_hist), in_hbm(jnp.swapaxes(greater_hist, 2, 3)))

    short = times // 4
    sizes = [(times - short) // 2, times - short - (times - short) // 2, short]
    chunks = len(sizes)

    def history(chunk, order):
        each = sizes[chunk]
        return list(pl.pallas_call(
            functools.partial(history_kernel, sum(sizes[:chunk])),
            out_shape=[
                pltpu.VMEM((slices, norb, each * 2 * width), jnp.bfloat16),
                pltpu.VMEM((slices, norb, each * 2 * width), jnp.bfloat16),
                pltpu.VMEM((norb, each * 2 * width), jnp.float32),
                pltpu.VMEM((2, each) + current_row.shape[2:], jnp.float32),
            ],
            in_specs=[SMEM] + [HBM] * 3,
            out_specs=[VMEM] * 4,
            scratch_shapes=[
                pltpu.VMEM((2, slices, each, norb, width), jnp.float32),
                pltpu.VMEM(adjacency.shape, jnp.int32),
                pltpu.SemaphoreType.DMA((each + 2,)),
            ],
            compiler_params=limit(12),
            cost_estimate=pl.CostEstimate(flops=0, bytes_accessed=64 * 1024, transcendentals=0),
            name=f"history_{chunk}",
        )(order, in_hbm(advanced_hist), in_hbm(current_row), in_hbm(adjacency)))

    def moved(x, target):
        pairs = [
            (r * ocol_size + c, target(r, c)[0] * ocol_size + target(r, c)[1])
            for r in range(orow_size)
            for c in range(ocol_size)
        ]
        return lax.ppermute(x, ("orow", "ocol"), pairs)

    def over_core(x):
        return moved(x, lambda r, c: (r, c ^ 1))

    def over_orow(x):
        return moved(x, lambda r, c: (r ^ 1, c))

    def over_ocol(x):
        return moved(x, lambda r, c: (r, c ^ 2))

    orow_early, ocol_late, orow_late, ocol_early = over_orow(early), over_ocol(late), over_orow(late), over_ocol(early)
    own_partner = over_core(sigma)
    histories = [history(0, me[0])]
    far_early, far_late, _ = lax.optimization_barrier((orow_early, ocol_late, histories[0][3]))
    far = [over_ocol(far_early), over_orow(far_late)]
    order = lax.optimization_barrier((me[0], far_early, histories[0][3]))[0]
    histories.append(history(1, order))
    orow_partner = [over_core(orow_early), over_core(orow_late)]
    ocol_partner = [over_core(ocol_early), over_core(ocol_late)]
    left_shape = (slices, orow_size, 2, ocol_size) + block[2:]
    *left, token = pl.pallas_call(
        functools.partial(assemble_kernel, ((0, 0), (0, 1), (1, 0), (0, 2), (1, 1), (0, 3))),
        out_shape=[pltpu.VMEM(left_shape, jnp.bfloat16)] * 2 + [pltpu.VMEM((8, 128), jnp.float32)],
        in_specs=[SMEM] * 2 + [VMEM] * 10,
        out_specs=[VMEM] * 3,
        compiler_params=limit(4),
        cost_estimate=pl.CostEstimate(flops=0, bytes_accessed=64 * 1024, transcendentals=0),
        name="assemble",
    )(*me[1:], *[in_vmem(x) for x in (sigma, own_partner, orow_early, orow_late, ocol_early, ocol_late, *orow_partner, *ocol_partner)])
    *far, _ = lax.optimization_barrier((*far, histories[1][3]))
    far_partner = [over_core(x) for x in far]
    late = {(1, 2): far, (1, 3): far_partner}

    rows = norb // hist_size
    ring = ring_of(hist_size) if hist_size <= 8 else []
    arrived, own, firsts = [], [], []
    for chunk, each in enumerate(sizes):
        if ring:
            out_shape = [pltpu.VMEM((2, each, rows, width), jnp.float32)] * hist_size
        else:
            out_shape = [pltpu.VMEM((2, each, norb, width), jnp.float32)]
        count, aliases, masks = len(out_shape), {}, ()
        if chunk >= 2:
            histories.append(history(chunk, lax.optimization_barrier((me[0], own[chunk - 1]))[0]))
        after = lax.optimization_barrier((me[0], firsts[chunk - 2]))[0] if chunk >= 2 and ring else me[0]
        operands = [after, *me[1:]] + [in_vmem(x) for x in histories[chunk][:3]] + [in_vmem(x) for x in left]
        if chunk == 0:
            masks = tuple(late)
            operands += [in_vmem(x) for pair in late.values() for x in pair]
            out_shape += [pltpu.VMEM(left_shape, jnp.bfloat16)] * 2
            aliases = {6: count, 7: count + 1}
        parts = pl.pallas_call(
            functools.partial(chunk_kernel, masks, ring),
            out_shape=out_shape,
            in_specs=[SMEM] * 3 + [VMEM] * (len(operands) - 3),
            out_specs=[VMEM] * len(out_shape),
            scratch_shapes=[pltpu.VMEM((each, hist_size, 2, rows, width), jnp.float32)],
            input_output_aliases=aliases,
            cost_estimate=pl.CostEstimate(
                flops=6 * each * slices * 2 * norb * norb * 2 * width, bytes_accessed=0, transcendentals=0
            ),
            compiler_params=limit(16),
            name=f"products_{chunk}",
        )(*operands)
        if chunk == 0:
            left, parts = parts[count:], parts[:count]
        if not ring:
            total = lax.psum_scatter(parts[0], "hist", scatter_dimension=2, tiled=True)
            arrived.append(total)
            own.append(jnp.zeros_like(total))
            continue
        pairs = [(ring[p], ring[(p + 1) % hist_size]) for p in range(hist_size)]
        moving = parts[0]
        for m in range(1, hist_size):
            moving = lax.ppermute(moving, "hist", pairs)
            if m == 1:
                firsts.append(moving)
            if m < hist_size - 1:
                moving = add(moving, parts[m])
        arrived.append(moving)
        own.append(parts[-1])
    return pl.pallas_call(
        step_kernel,
        out_shape=jax.ShapeDtypeStruct(current_row.shape, jnp.float32),
        in_specs=[VMEM] * (3 * chunks),
        out_specs=HBM,
        scratch_shapes=[pltpu.VMEM(current_row.shape, jnp.float32), pltpu.SemaphoreType.DMA((chunks,))],
        compiler_params=limit(4),
        name="step",
    )(*[in_vmem(x) for x in arrived + own + [h[3] for h in histories]])


def solution(mesh):
    in_specs = (
        P(None, "hist", "ocol", "orow"),
        P(None, "hist", "orow", "ocol"),
        P(None, "hist", "ocol", None, "orow"),
        P(None, "ocol", "hist", "orow"),
        P("hist", None),
        P("hist"),
        P(),
    )
    out_specs = P(None, "ocol", "hist", "orow")
    body = functools.partial(on_device, mesh.shape["hist"], mesh.shape["orow"], mesh.shape["ocol"])
    return jax.shard_map(
        body, mesh=mesh, in_specs=in_specs, out_specs=out_specs, check_vma=False
    )
```

```python
import functools

import jax
import jax.numpy as jnp
from jax import lax
from jax.experimental import pallas as pl
from jax.experimental.pallas import tpu as pltpu
from jax.sharding import PartitionSpec as P

coupling_square = 0.25
hopping = 4.0
time_step = 0.01
VMEM = pl.BlockSpec(memory_space=pltpu.VMEM)
SMEM = pl.BlockSpec(memory_space=pltpu.SMEM)
HBM = pl.BlockSpec(memory_space=pltpu.HBM)


def sigma_kernel(hist_ref, orow_ref, ocol_ref, step_ref, table_hbm, lesser_hbm, greater_hbm, out_ref, early_ref, late_ref, lesser, greater, table_ref, sems):
    slices = lesser.shape[1]
    copies = [
        pltpu.make_async_copy(source, target, sems.at[place])
        for place, (source, target) in enumerate(
            [(table_hbm, table_ref), (lesser_hbm, lesser), (greater_hbm, greater)]
        )
    ]
    for copy in copies:
        copy.start()
    for copy in copies:
        copy.wait()
    for s in range(slices):
        numerator = jnp.full((1, lesser.shape[3]), table_ref[s], jnp.int32).astype(jnp.float32)
        weight = jnp.where(hist_ref[0] * slices + s <= step_ref[0], numerator / 24.0, 0.0)
        a_re, a_im = lesser[0, s], lesser[1, s]
        b_re, b_im = greater[0, s], greater[1, s]
        square_re = a_re * a_re - a_im * a_im
        square_im = 2.0 * a_re * a_im
        scale = coupling_square * weight
        half = early_ref.shape[1]
        part_ref = early_ref if s < half else late_ref
        for part, value in enumerate((square_re * b_re - square_im * b_im, square_re * b_im + square_im * b_re)):
            out_ref[part, s] = scale * value
            part_ref[part, s % half] = scale * value


def split(x):
    high = x.astype(jnp.bfloat16)
    return high, (x - high.astype(jnp.float32)).astype(jnp.bfloat16)


def history_kernel(
    first, order_ref, advanced_hbm, row_hbm, adjacency_hbm, high_ref, low_ref, hop_ref, row, advanced, adjacency, sems
):
    slices, each, width = advanced.shape[1], advanced.shape[2], advanced.shape[4]
    near = [
        pltpu.make_async_copy(row_hbm.at[:, pl.ds(first, each)], row, sems.at[each]),
        pltpu.make_async_copy(adjacency_hbm, adjacency, sems.at[each + 1]),
    ]
    far = [
        pltpu.make_async_copy(advanced_hbm.at[:, :, first + t], advanced.at[:, :, t], sems.at[t]) for t in range(each)
    ]
    for copy in near + far:
        copy.start()
    for copy in near:
        copy.wait()
    graph = (-hopping * adjacency[...].astype(jnp.float32)).T.astype(jnp.bfloat16)
    for t in range(each):
        place = t * 2 * width
        row_high, row_low = split(jnp.concatenate([row[0, t], row[1, t]], axis=1))
        hop_ref[:, place : place + 2 * width] = jnp.dot(
            graph, row_high, preferred_element_type=jnp.float32
        ) + jnp.dot(graph, row_low, preferred_element_type=jnp.float32)
    for t in range(each):
        far[t].wait()
        for s in range(slices):
            for part in range(2):
                place = (2 * t + part) * width
                high, low = split(advanced[part, s, t])
                high_ref[s, :, place : place + width] = high
                low_ref[s, :, place : place + width] = low


def assemble(masks, my_orow, my_ocol, blocks, left_high, left_low):
    for (flip_orow, flip_ocol), block in zip(masks, blocks):
        at_orow = jnp.bitwise_xor(my_orow, flip_orow)
        at_ocol = jnp.bitwise_xor(my_ocol, flip_ocol)
        for s in range(left_high.shape[0]):
            for part in range(2):
                high, low = split(block(part, s) if callable(block) else block[part, s])
                left_high[s, at_orow, part, at_ocol] = high
                left_low[s, at_orow, part, at_ocol] = low


def assemble_kernel(masks, orow_ref, ocol_ref, own, own_partner, *refs):
    halves, (left_high, left_low, token) = refs[:-3], refs[-3:]
    blocks = [own, own_partner] + [join(halves[2 * place : 2 * place + 2]) for place in range(len(halves) // 2)]
    assemble(masks, orow_ref[0], ocol_ref[0], blocks, left_high, left_low)
    token[...] = jnp.zeros_like(token)


def join(halves):
    half = halves[0].shape[1]
    return lambda part, s: halves[s // half][part, s % half]


def chunk_kernel(masks, ring, hist_ref, orow_ref, ocol_ref, right_high, right_low, hop_ref, left_high, left_low, *refs):
    outs, result = refs[2 * len(masks) : -1], refs[-1]
    if masks:
        left_high, left_low, outs = outs[-2], outs[-1], outs[:-2]
        blocks = [join(refs[2 * place : 2 * place + 2]) for place in range(len(masks))]
        assemble(masks, orow_ref[0], ocol_ref[0], blocks, left_high, left_low)
    slices, halves = left_high.shape[:2]
    norb = right_high.shape[1]
    width = outs[0].shape[3]

    def left(ref, s):
        return jnp.concatenate([ref[s, half].reshape(2 * norb, norb // halves) for half in range(halves)], axis=1)

    total = None
    for s in range(slices):
        high = right_high[s]
        here = jnp.dot(
            jnp.concatenate([left(left_high, s), left(left_high, s), left(left_low, s)], axis=1),
            jnp.concatenate([high, right_low[s], high], axis=0),
            preferred_element_type=jnp.float32,
        )
        total = here if total is None else total + here
    for t in range(outs[0].shape[1]):
        at = 2 * width * t
        sum_re = total[:norb, at : at + width] - total[norb:, at + width : at + 2 * width] + hop_ref[:, at : at + width]
        sum_im = total[:norb, at + width : at + 2 * width] + total[norb:, at : at + width] + hop_ref[:, at + width : at + 2 * width]
        if not ring:
            outs[0][0, t] = sum_re
            outs[0][1, t] = sum_im
            continue
        rows = norb // len(ring)
        for block in range(len(ring)):
            result[t, block, 0] = sum_re[block * rows : (block + 1) * rows]
            result[t, block, 1] = sum_im[block * rows : (block + 1) * rows]
    if not ring:
        return
    size = len(ring)
    my_hist = hist_ref[0]
    my_place = sum(jnp.where(my_hist == h, ring.index(h), 0) for h in range(size))
    for step, out in enumerate(outs):
        place = my_place + (size - 1 - step)
        place = jnp.where(place >= size, place - size, place)
        block = sum(jnp.where(place == p, ring[p], 0) for p in range(size))
        for t in range(out.shape[1]):
            out[0, t] = result[t, block, 0]
            out[1, t] = result[t, block, 1]


def step_kernel(*refs):
    chunks = (len(refs) - 3) // 3
    arrived, own, row = refs[:chunks], refs[chunks : 2 * chunks], refs[2 * chunks : 3 * chunks]
    out_hbm, out, sems = refs[3 * chunks :]
    copies, first = [], 0
    for chunk in range(chunks):
        here = pl.ds(first, own[chunk].shape[1])
        first += own[chunk].shape[1]
        out[0, here] = row[chunk][0] + time_step * (arrived[chunk][1] + own[chunk][1])
        out[1, here] = row[chunk][1] - time_step * (arrived[chunk][0] + own[chunk][0])
        copies.append(pltpu.make_async_copy(out.at[:, here], out_hbm.at[:, here], sems.at[chunk]))
        copies[-1].start()
    for copy in copies:
        copy.wait()


def ring_of(size):
    return [place for place in range(size) if place == 0 or place % 2 == 1] + [
        place for place in range(size - 1, 0, -1) if place % 2 == 0
    ]


def limit(mebibytes):
    return pltpu.CompilerParams(vmem_limit_bytes=mebibytes * 1024 * 1024)


def in_vmem(x):
    return pltpu.with_memory_space_constraint(x, pltpu.VMEM)


def in_hbm(x):
    return pltpu.with_memory_space_constraint(x, pltpu.HBM)


def add_kernel(left_ref, right_ref, out_ref):
    out_ref[...] = left_ref[...] + right_ref[...]


def add(left, right):
    return pl.pallas_call(
        add_kernel,
        out_shape=pltpu.VMEM(left.shape, left.dtype),
        in_specs=[VMEM] * 2,
        out_specs=VMEM,
        compiler_params=limit(4),
        name="add",
    )(in_vmem(left), in_vmem(right))


def on_device(
    hist_size, orow_size, ocol_size, lesser_hist, greater_hist, advanced_hist, current_row, adjacency, weight_table, step_index
):
    slices, times, norb, width = advanced_hist.shape[1:]
    block = lesser_hist.shape
    my_hist, my_orow, my_ocol = lax.axis_index("hist"), lax.axis_index("orow"), lax.axis_index("ocol")
    me = [index.reshape(1).astype(jnp.int32) for index in (my_hist, my_orow, my_ocol)]
    half_shape = (2, slices // 2) + block[2:]
    sigma, early, late = pl.pallas_call(
        sigma_kernel,
        out_shape=[pltpu.VMEM(shape, jnp.float32) for shape in (block, half_shape, half_shape)],
        in_specs=[SMEM] * 4 + [HBM] * 3,
        out_specs=[VMEM] * 3,
        scratch_shapes=[
            pltpu.VMEM(block, jnp.float32),
            pltpu.VMEM(block, jnp.float32),
            pltpu.SMEM(weight_table.shape, jnp.int32),
            pltpu.SemaphoreType.DMA((3,)),
        ],
        compiler_params=limit(4),
        name="sigma",
    )(*me, step_index, in_hbm(weight_table), in_hbm(lesser_hist), in_hbm(jnp.swapaxes(greater_hist, 2, 3)))

    short = times // 4
    sizes = [(times - short) // 2, short, times - short - (times - short) // 2]
    chunks = len(sizes)

    def history(chunk, order):
        each = sizes[chunk]
        return list(pl.pallas_call(
            functools.partial(history_kernel, sum(sizes[:chunk])),
            out_shape=[
                pltpu.VMEM((slices, norb, each * 2 * width), jnp.bfloat16),
                pltpu.VMEM((slices, norb, each * 2 * width), jnp.bfloat16),
                pltpu.VMEM((norb, each * 2 * width), jnp.float32),
                pltpu.VMEM((2, each) + current_row.shape[2:], jnp.float32),
            ],
            in_specs=[SMEM] + [HBM] * 3,
            out_specs=[VMEM] * 4,
            scratch_shapes=[
                pltpu.VMEM((2, slices, each, norb, width), jnp.float32),
                pltpu.VMEM(adjacency.shape, jnp.int32),
                pltpu.SemaphoreType.DMA((each + 2,)),
            ],
            compiler_params=limit(12),
            cost_estimate=pl.CostEstimate(flops=0, bytes_accessed=64 * 1024, transcendentals=0),
            name=f"history_{chunk}",
        )(order, in_hbm(advanced_hist), in_hbm(current_row), in_hbm(adjacency)))

    def moved(x, target):
        pairs = [
            (r * ocol_size + c, target(r, c)[0] * ocol_size + target(r, c)[1])
            for r in range(orow_size)
            for c in range(ocol_size)
        ]
        return lax.ppermute(x, ("orow", "ocol"), pairs)

    def over_core(x):
        return moved(x, lambda r, c: (r, c ^ 1))

    def over_orow(x):
        return moved(x, lambda r, c: (r ^ 1, c))

    def over_ocol(x):
        return moved(x, lambda r, c: (r, c ^ 2))

    orow_early, ocol_late, orow_late, ocol_early = over_orow(early), over_ocol(late), over_orow(late), over_ocol(early)
    own_partner = over_core(sigma)
    histories = [history(0, me[0])]
    far_early, far_late, _ = lax.optimization_barrier((orow_early, ocol_late, histories[0][3]))
    far = [over_ocol(far_early), over_orow(far_late)]
    order = lax.optimization_barrier((me[0], far_early, histories[0][3]))[0]
    histories.append(history(1, order))
    orow_partner = [over_core(orow_early), over_core(orow_late)]
    ocol_partner = [over_core(ocol_early), over_core(ocol_late)]
    left_shape = (slices, orow_size, 2, ocol_size) + block[2:]
    *left, token = pl.pallas_call(
        functools.partial(assemble_kernel, ((0, 0), (0, 1), (1, 0), (0, 2), (1, 1), (0, 3))),
        out_shape=[pltpu.VMEM(left_shape, jnp.bfloat16)] * 2 + [pltpu.VMEM((8, 128), jnp.float32)],
        in_specs=[SMEM] * 2 + [VMEM] * 10,
        out_specs=[VMEM] * 3,
        compiler_params=limit(4),
        cost_estimate=pl.CostEstimate(flops=0, bytes_accessed=64 * 1024, transcendentals=0),
        name="assemble",
    )(*me[1:], *[in_vmem(x) for x in (sigma, own_partner, orow_early, orow_late, ocol_early, ocol_late, *orow_partner, *ocol_partner)])
    *far, _ = lax.optimization_barrier((*far, histories[1][3]))
    far_partner = [over_core(x) for x in far]
    late = {(1, 2): far, (1, 3): far_partner}

    rows = norb // hist_size
    ring = ring_of(hist_size) if hist_size <= 8 else []
    arrived, own, firsts = [], [], []
    for chunk, each in enumerate(sizes):
        if ring:
            out_shape = [pltpu.VMEM((2, each, rows, width), jnp.float32)] * hist_size
        else:
            out_shape = [pltpu.VMEM((2, each, norb, width), jnp.float32)]
        count, aliases, masks = len(out_shape), {}, ()
        if chunk >= 2:
            histories.append(history(chunk, lax.optimization_barrier((me[0], own[chunk - 1]))[0]))
        after = lax.optimization_barrier((me[0], firsts[chunk - 2]))[0] if chunk >= 2 and ring else me[0]
        operands = [after, *me[1:]] + [in_vmem(x) for x in histories[chunk][:3]] + [in_vmem(x) for x in left]
        if chunk == 0:
            masks = tuple(late)
            operands += [in_vmem(x) for pair in late.values() for x in pair]
            out_shape += [pltpu.VMEM(left_shape, jnp.bfloat16)] * 2
            aliases = {6: count, 7: count + 1}
        parts = pl.pallas_call(
            functools.partial(chunk_kernel, masks, ring),
            out_shape=out_shape,
            in_specs=[SMEM] * 3 + [VMEM] * (len(operands) - 3),
            out_specs=[VMEM] * len(out_shape),
            scratch_shapes=[pltpu.VMEM((each, hist_size, 2, rows, width), jnp.float32)],
            input_output_aliases=aliases,
            cost_estimate=pl.CostEstimate(
                flops=6 * each * slices * 2 * norb * norb * 2 * width, bytes_accessed=0, transcendentals=0
            ),
            compiler_params=limit(16),
            name=f"products_{chunk}",
        )(*operands)
        if chunk == 0:
            left, parts = parts[count:], parts[:count]
        if not ring:
            total = lax.psum_scatter(parts[0], "hist", scatter_dimension=2, tiled=True)
            arrived.append(total)
            own.append(jnp.zeros_like(total))
            continue
        pairs = [(ring[p], ring[(p + 1) % hist_size]) for p in range(hist_size)]
        moving = parts[0]
        for m in range(1, hist_size):
            moving = lax.ppermute(moving, "hist", pairs)
            if m == 1:
                firsts.append(moving)
            if m < hist_size - 1:
                moving = add(moving, parts[m])
        arrived.append(moving)
        own.append(parts[-1])
    return pl.pallas_call(
        step_kernel,
        out_shape=jax.ShapeDtypeStruct(current_row.shape, jnp.float32),
        in_specs=[VMEM] * (3 * chunks),
        out_specs=HBM,
        scratch_shapes=[pltpu.VMEM(current_row.shape, jnp.float32), pltpu.SemaphoreType.DMA((chunks,))],
        compiler_params=limit(4),
        name="step",
    )(*[in_vmem(x) for x in arrived + own + [h[3] for h in histories]])


def solution(mesh):
    in_specs = (
        P(None, "hist", "ocol", "orow"),
        P(None, "hist", "orow", "ocol"),
        P(None, "hist", "ocol", None, "orow"),
        P(None, "ocol", "hist", "orow"),
        P("hist", None),
        P("hist"),
        P(),
    )
    out_specs = P(None, "ocol", "hist", "orow")
    body = functools.partial(on_device, mesh.shape["hist"], mesh.shape["orow"], mesh.shape["ocol"])
    return jax.shard_map(
        body, mesh=mesh, in_specs=in_specs, out_specs=out_specs, check_vma=False
    )
```
